256 devices in a mesh: mirror: 4 (over x), expert: 64 (over y, z, core).
Axes of the slice: x: 4, y: 4, z: 8, core: 2. Of those that a mesh axis runs over, the one named last changes fastest.
Arguments:
- tokens: bfloat16 [32768, 1536], P(('mirror', 'expert')), may hold values from -6 to 6
- routes: int32 [32768, 8], P(('mirror', 'expert')), may hold values from 0 to 63, all different within a row; in each aligned block of 128 rows (0 to 127, 128 to 255, ...) at most 20 rows name the same one
- gate_probs: float32 [32768, 8], P(('mirror', 'expert')), may hold values from 0.05 to 0.3
- cotangent: bfloat16 [32768, 1536], P(('mirror', 'expert')), may hold values from -1.5 to 1.5
- w_gate: bfloat16 [64, 1536, 384], P('expert'), may hold values from -0.15625 to 0.15625
- w_up: bfloat16 [64, 1536, 384], P('expert'), may hold values from -0.15625 to 0.15625
- w_down: bfloat16 [64, 384, 1536], P('expert'), may hold values from -0.3125 to 0.3125
Outputs:
- layer_out: bfloat16 [32768, 1536], P(('mirror', 'expert'))
- grad_tokens: bfloat16 [32768, 1536], P(('mirror', 'expert'))
- grad_probs: float32 [32768, 8], P(('mirror', 'expert'))
- grad_w_gate: float32 [64, 1536, 384], P('expert', 'mirror')
- grad_w_up: float32 [64, 1536, 384], P('expert', 'mirror')
- grad_w_down: float32 [64, 384, 1536], P('expert', None, 'mirror')
The draws below stay inside these ranges and needn't reach their ends.
Inputs may be any that keep to these rules, and one draw needn't show every extreme that they name: `routes`: each row names 8 different experts. In the rows of one device no expert is named more than 20 times, and in every draw some device has an expert named exactly 20 times.
All inputs are finite; a program needn't handle non-finite values.
Results may differ from the reference program's by a relative error of at most 0.012.
Values may be sent and summed in bfloat16 or wider, within the bound.
A program may use at most 128 MiB of HBM per device.

```python
import math
import jax
import jax.numpy as jnp
import numpy as np
from jax import lax

D = 1536
F = 384
TOP = 8
TOK_DEV = 128
EXPERTS = 64
CAP = 20
TOKENS = 32768
N_MIRROR = 4
N_EXPERT = 64


def shard_levels(rng, dims, cuts, smallest, high):
    loudness, own = 1.0, jax.random.fold_in(rng, 6)
    for dim, blocks in cuts:
        draws = jnp.exp(jax.random.uniform(jax.random.fold_in(own, dim), (blocks,), jnp.float32, smallest / len(cuts), high / len(cuts)))
        loudness = loudness * jnp.repeat(draws, dims[dim] // blocks).reshape([-1 if axis == dim else 1 for axis in range(len(dims))])
    return loudness


def assign_block(stream_key, own, number, rows, number_of, top, bound, lean):
    sequence = jax.random.permutation(stream_key, number_of)
    crowded, common = load_shares(number_of, rows * top, bound, lean, True), load_shares(number_of, rows * top, bound, lean, False)
    places = jnp.arange(number_of)

    def named(sizes, offset_by):
        used = int((sizes > 0).sum())
        fixed = max(1, used // 4)
        moved = fixed + (places - fixed + offset_by * (used - fixed)) % max(1, number_of - fixed)
        return jnp.zeros((number_of,), jnp.int32).at[sequence[jnp.where(places < fixed, places, moved)]].set(jnp.asarray(sizes, jnp.int32))

    sizes = jnp.where(number % 4 == 0, named(crowded, number // 4), named(common, number - number // 4 - 1))
    mixed = jax.random.permutation(jax.random.fold_in(own, 3), number_of)
    source_of, taker = mixed[0:number_of // 2 * 2:2], mixed[1:number_of // 2 * 2:2]
    slack = jnp.minimum(sizes[source_of] - 1, bound - sizes[taker]) // 2
    slack = jnp.where((source_of == sequence[0]) | (taker == sequence[0]) | (sizes[taker] == 0), 0, jnp.maximum(slack, 0))
    moved = jax.random.randint(jax.random.fold_in(own, 4), (number_of // 2,), 0, 1 << 20) % (slack + 1)
    sizes = sizes.at[source_of].add(-moved).at[taker].add(moved)
    members = jnp.searchsorted(jnp.cumsum(sizes), jnp.arange(rows * top), side="right").astype(jnp.int32)
    grid = members.reshape(top, rows).T
    grid = grid[jax.random.permutation(jax.random.fold_in(own, 1), rows)]
    offset_by = jax.random.randint(jax.random.fold_in(own, 2), (rows, 1), 0, top)
    return jnp.take_along_axis(grid, (jnp.arange(top)[None, :] + offset_by) % top, axis=1)


def load_shares(count, total, most, slope, full):
    weights = [(1 << 20) // math.isqrt(grade ** slope) + 1 for grade in range(1, count + 1)]
    largest = most if full else min(most, max(-(-total // count), total * weights[0] // sum(weights)))
    least = 1 if total - largest >= count - 1 else 0
    given, spare = [largest] + [least] * (count - 1), total - largest - least * (count - 1)
    while spare > 0:
        movable = [i for i in range(1, count) if given[i] < largest] or [i for i in range(1, count) if given[i] < most]
        mass, remaining = sum([weights[i] for i in movable]), spare
        for i in movable:
            more = min(most - given[i], max(1, remaining * weights[i] // mass), spare)
            given[i] = given[i] + more
            spare = spare - more
    return np.array(given)


def bell_draw(own_key, extent, spread, limit, cuts=(), kind=jnp.bfloat16):
    values = spread * jax.random.normal(own_key, extent, jnp.float32)
    if cuts:
        values = values * shard_levels(own_key, extent, cuts, -0.22, 0.18)
    return jnp.clip(values, -limit, limit).astype(kind)


def setup_inputs(seed: int = 0) -> dict:
    key_list = jax.random.split(jax.random.key(seed), 8)
    tokens = bell_draw(key_list[0], (TOKENS, D), 1.0, 6.0, ((0, 256),))
    routes_keys = jax.random.split(jax.random.fold_in(key_list[1], 1), TOKENS // TOK_DEV)
    routes_turns = jax.random.permutation(jax.random.fold_in(key_list[1], 3), TOKENS // TOK_DEV)
    routes = jax.vmap(lambda own, number: assign_block(jax.random.fold_in(key_list[1], 2), own, number, TOK_DEV, EXPERTS, TOP, CAP, 2))(routes_keys, routes_turns).reshape((TOKENS, TOP))
    gate_probs = jnp.clip(0.05 + 0.25 * jax.random.uniform(key_list[2], (TOKENS, TOP), jnp.float32) ** shard_levels(key_list[2], (TOKENS, TOP), ((0, 256),), -0.2, 0.2), 0.05, 0.3)
    cotangent = bell_draw(key_list[3], (TOKENS, D), 0.25, 1.5, ((0, 256),))
    w_gate = bell_draw(key_list[4], (EXPERTS, D, F), D ** -0.5, 0.15625, ((0, 64),))
    w_up = bell_draw(key_list[5], (EXPERTS, D, F), D ** -0.5, 0.15625, ((0, 64),))
    w_down = bell_draw(key_list[6], (EXPERTS, F, D), F ** -0.5, 0.3125, ((0, 64),))
    return dict(tokens=tokens, routes=routes, gate_probs=gate_probs, cotangent=cotangent, w_gate=w_gate, w_up=w_up, w_down=w_down)


def reference(tokens, routes, gate_probs, cotangent, w_gate, w_up, w_down):
    group = TOK_DEV * N_EXPERT
    route_total = group * TOP
    rows_max = N_EXPERT * CAP
    outs_mixed = []
    outs_grad = []
    outs_probs = []
    sum_gate = jnp.zeros((EXPERTS, D, F), jnp.float32)
    sum_up = jnp.zeros((EXPERTS, D, F), jnp.float32)
    sum_down = jnp.zeros((EXPERTS, F, D), jnp.float32)
    for mirror_index in range(N_MIRROR):
        lower = mirror_index * group
        inputs = tokens[lower:lower + group]
        flat_routes = routes[lower:lower + group].reshape(route_total)
        flat_probs = gate_probs[lower:lower + group].reshape(route_total)
        grads_out = cotangent[lower:lower + group]
        route_range = jnp.arange(route_total, dtype=jnp.int32)

        def per_expert(totals, expert_id):
            mixed_acc, grad_acc, probs_acc = totals
            matches = flat_routes == expert_id
            position = jnp.cumsum(matches.astype(jnp.int32)) - 1
            targets = jnp.where(matches, position, rows_max).astype(jnp.int32)
            route_ids = jnp.full((rows_max,), route_total, jnp.int32).at[targets].set(route_range, mode="drop")
            valid_rows = route_ids < route_total
            safe_ids = jnp.where(valid_rows, route_ids, 0).astype(jnp.int32)
            token_ids = (safe_ids // TOP).astype(jnp.int32)
            expert_rows = jnp.where(valid_rows[:, None], inputs[token_ids], jnp.zeros((), jnp.bfloat16)).astype(jnp.bfloat16)
            gate_mat = w_gate[expert_id]
            up_mat = w_up[expert_id]
            down_mat = w_down[expert_id]
            pre_gate = jnp.dot(expert_rows, gate_mat, preferred_element_type=jnp.float32)
            pre_up = jnp.dot(expert_rows, up_mat, preferred_element_type=jnp.float32)
            sigmoid_gate = jax.nn.sigmoid(pre_gate)
            hidden = (pre_gate * sigmoid_gate * pre_up).astype(jnp.bfloat16)
            expert_out = jnp.dot(hidden, down_mat, preferred_element_type=jnp.float32).astype(jnp.bfloat16)
            prob_rows = jnp.where(valid_rows, flat_probs[safe_ids], jnp.zeros((), jnp.float32))
            mixed_acc = mixed_acc.at[token_ids].add(prob_rows[:, None] * expert_out.astype(jnp.float32))
            grad_rows_in = grads_out[token_ids]
            route_grad = jnp.sum(grad_rows_in.astype(jnp.float32) * expert_out.astype(jnp.float32), axis=1)
            probs_acc = probs_acc.at[jnp.where(valid_rows, safe_ids, route_total).astype(jnp.int32)].set(route_grad, mode="drop")
            scaled_rows = (prob_rows[:, None] * grad_rows_in.astype(jnp.float32)).astype(jnp.bfloat16)
            grad_hidden = jnp.dot(scaled_rows, down_mat.T, preferred_element_type=jnp.float32)
            grad_pre_gate = (grad_hidden * pre_up * sigmoid_gate * (1.0 + pre_gate * (1.0 - sigmoid_gate))).astype(jnp.bfloat16)
            grad_pre_up = (grad_hidden * pre_gate * sigmoid_gate).astype(jnp.bfloat16)
            grad_route = (jnp.dot(grad_pre_gate, gate_mat.T, preferred_element_type=jnp.float32)
                          + jnp.dot(grad_pre_up, up_mat.T, preferred_element_type=jnp.float32)).astype(jnp.bfloat16)
            grad_acc = grad_acc.at[token_ids].add(grad_route.astype(jnp.float32))
            part_gate = jnp.dot(expert_rows.T, grad_pre_gate, preferred_element_type=jnp.float32)
            part_up = jnp.dot(expert_rows.T, grad_pre_up, preferred_element_type=jnp.float32)
            part_down = jnp.dot(hidden.T, scaled_rows, preferred_element_type=jnp.float32)
            return (mixed_acc, grad_acc, probs_acc), (part_gate, part_up, part_down)

        start_totals = (jnp.zeros((group, D), jnp.float32), jnp.zeros((group, D), jnp.float32),
                        jnp.zeros((route_total,), jnp.float32))
        totals, parts = lax.scan(per_expert, start_totals, jnp.arange(EXPERTS, dtype=jnp.int32))
        outs_mixed.append(totals[0].astype(jnp.bfloat16))
        outs_grad.append(totals[1].astype(jnp.bfloat16))
        outs_probs.append(totals[2].reshape(group, TOP))
        rounded = lax.optimization_barrier((parts[0].astype(jnp.bfloat16), parts[1].astype(jnp.bfloat16),
                                            parts[2].astype(jnp.bfloat16)))
        sum_gate = sum_gate + rounded[0].astype(jnp.float32)
        sum_up = sum_up + rounded[1].astype(jnp.float32)
        sum_down = sum_down + rounded[2].astype(jnp.float32)
    return (jnp.concatenate(outs_mixed, 0), jnp.concatenate(outs_grad, 0), jnp.concatenate(outs_probs, 0),
            sum_gate, sum_up, sum_down)
```

```python
import jax
import jax.numpy as jnp
from jax import lax
from jax.experimental import pallas as pl
from jax.experimental.pallas import tpu as pltpu
from jax.sharding import PartitionSpec as P

MESH = pl.DeviceIdType.MESH
F32 = jnp.float32
BF16 = jnp.bfloat16
NX, NY, NZ, NJ = 4, 4, 8, 8
T = 128
CAP = 20
Q = 4
DQ = 384
BLK = Q * CAP
R = NJ * BLK
TQ = Q * T
F = 384
D = 1536
ROWS = NJ * CAP
BATCH = 2 * ROWS
WROWS = F + F // 2


def dot(a, b):
    return jnp.dot(a, b, preferred_element_type=F32)


def dot_nt(a, b):
    return lax.dot_general(a, b, (((1,), (1,)), ((), ())), preferred_element_type=F32)


def dot_tn(a, b):
    return lax.dot_general(a, b, (((0,), (0,)), ((), ())), preferred_element_type=F32)


def dot_f32(a, b):
    return jnp.dot(a, b, preferred_element_type=F32, precision=lax.Precision.HIGHEST)


def iota(shape, dim):
    return lax.broadcasted_iota(jnp.int32, shape, dim)


def div20(v):
    return (v * 3277) >> 16


def wait(ref, sem):
    pltpu.make_async_copy(ref, ref, sem).wait()


def kernel(
    routes_ref, probs_ref, tok_ref, cot_ref, wg_hbm, wu_hbm, wd_hbm,
    out_ref, gtok_ref, gprob_ref, ogate_ref, oup_ref, odown_ref,
    wg, wu, wd, held, sent, rows_in, rows_back, xs, ss, hid, zback, wpart, perm, perm_t, psum,
    meta, meta_in, gs, gp_a, gp_b, gp_c, gp_d,
    w_sem, z_send, z_recv, m_send, m_recv, y_send, y_recv, r_send, r_recv,
    b_send, b_recv, x_send, x_recv, g_send, g_recv,
):
    mx = lax.axis_index("mirror")
    e = lax.axis_index("expert")
    y, z, core = e // 16, (e // 2) % 8, e % 2
    j = y * 2 + core

    def dev_j(other):
        return (mx, (other // 2) * 16 + z * 2 + other % 2)

    def dev_z(step):
        return (mx, y * 16 + ((z + step + 8) % 8) * 2 + core)

    def dev_x(step):
        return ((mx + step) % 4, e)

    offsets = [0, -1, 1, -2, 2, -3, 3, -4]

    barrier = pltpu.get_barrier_semaphore()
    for k in range(1, 8):
        pl.semaphore_signal(barrier, inc=1, device_id=dev_j((j + k) % 8), device_id_type=MESH)
        pl.semaphore_signal(barrier, inc=1, device_id=dev_z(k), device_id_type=MESH)
    for k in range(1, 4):
        pl.semaphore_signal(barrier, inc=1, device_id=dev_x(k), device_id_type=MESH)

    weights = [
        pltpu.make_async_copy(src, dst, w_sem.at[n])
        for n, (src, dst) in enumerate(((wg_hbm, wg), (wu_hbm, wu), (wd_hbm, wd)))
    ]
    for copy in weights:
        copy.start()

    for q in range(Q):
        held[0, 0, q * T : (q + 1) * T, :] = tok_ref[:, q * DQ : (q + 1) * DQ]
        held[0, 1, q * T : (q + 1) * T, :] = cot_ref[:, q * DQ : (q + 1) * DQ]

    row = iota((64, T), 0)
    expert = (((row & 7) >> 1) << 4) + ((row >> 3) << 1) + (row & 1)
    member = jnp.zeros((64, T), F32)
    weight = jnp.zeros((64, T), F32)
    for k in range(8):
        hit = routes_ref[k : k + 1, :] == expert
        member = member + jnp.where(hit, 1.0, 0.0)
        weight = weight + jnp.where(hit, probs_ref[k : k + 1, :], 0.0)
    before = jnp.where(iota((T, T), 0) < iota((T, T), 1), 1.0, 0.0).astype(BF16)
    rank = dot(member.astype(BF16), before)
    code = jnp.where(member > 0.5, rank, -1.0)
    for p in range(NZ):
        meta[p, 0:8, :] = code[p * 8 : (p + 1) * 8, :]
        meta[p, 8:16, :] = weight[p * 8 : (p + 1) * 8, :]
    meta_in[0] = meta[z]

    pl.semaphore_wait(barrier, 17)

    def remote(src, dst, send, recv, device):
        return pltpu.make_async_remote_copy(
            src_ref=src, dst_ref=dst, send_sem=send, recv_sem=recv, device_id=device, device_id_type=MESH
        )

    for a in range(2):
        for slot, step in ((1, 1), (2, -1)):
            remote(held.at[0, a], held.at[slot, a], z_send.at[0], z_recv.at[slot, a], dev_z(step)).start()
        if a == 0:
            for i in range(1, 8):
                to = -offsets[i]
                remote(
                    meta.at[(z + to + 8) % 8], meta_in.at[i], m_send.at[i], m_recv.at[i], dev_z(to)
                ).start()

    lane = iota((R, R), 1)
    r = iota((R, R), 0)
    r20 = div20(r)
    slot_of = r - r20 * 20
    perm[...] = jnp.where(lane == (r20 & 7) * BLK + (r20 >> 3) * CAP + slot_of, 1.0, 0.0).astype(BF16)
    perm_t[...] = jnp.where(
        lane == (r20 & 3) * ROWS + (r20 >> 2) * CAP + slot_of, 1.0, 0.0
    ).astype(BF16)

    r80 = iota((BLK, T), 0)
    q80 = div20(r80)
    slot80 = (r80 - q80 * CAP).astype(F32)

    def select(i, weighted):
        tops, lows = [], []
        for n in range(NJ):
            hit = meta_in[i, n : n + 1, :] == slot80
            if weighted:
                value = jnp.where(hit, meta_in[i, 8 + n : 9 + n, :], 0.0)
            else:
                value = jnp.where(hit, 1.0, 0.0)
            parts = [jnp.where(q80 == q, value, 0.0) for q in range(Q)]
            block = jnp.concatenate(parts, axis=1)
            top = block.astype(BF16)
            tops.append(top)
            if weighted:
                lows.append((block - top.astype(F32)).astype(BF16))
        top = jnp.concatenate(tops, axis=0)
        return (top, jnp.concatenate(lows, axis=0)) if weighted else (top,)

    def unit(i, a):
        s = i % 4

        @pl.when(i >= 1)
        def _():
            wait(held.at[i, a], z_recv.at[i, a])

        @pl.when((i >= 1) & (i <= 4))
        def _():
            step = 2 * (i % 2) - 1
            remote(held.at[i, a], held.at[i + 2, a], z_send.at[i], z_recv.at[i + 2, a], dev_z(step)).start()

        @pl.when(i == 5)
        def _():
            half = held.at[5, a, pl.ds(0, 256)]
            remote(half, held.at[7, a, pl.ds(0, 256)], z_send.at[5], z_recv.at[7, a], dev_z(1)).start()

        @pl.when(i == 6)
        def _():
            half = held.at[6, a, pl.ds(256, 256)]
            remote(half, held.at[7, a, pl.ds(256, 256)], z_send.at[6], z_recv.at[7, a], dev_z(-1)).start()

        if a == 0:

            @pl.when(i >= 1)
            def _():
                wait(meta_in.at[i], m_recv.at[i])

        source = held[i, a]
        picked = sum(dot(m, source) for m in select(i, a == 1))

        @pl.when(i >= 4)
        def _():
            wait(sent.at[s, a, pl.ds(0, 7 * BLK)], y_send.at[s, a])

        sent[s, a] = picked.astype(BF16)
        mine = pl.ds(pl.multiple_of(j * BLK, 16), BLK)
        rows_in[i, a, mine, :] = sent[s, a, mine, :]

        def send(k, _):
            other = (j + k) % 8
            theirs = pl.ds(pl.multiple_of(other * BLK, 16), BLK)
            remote(
                sent.at[s, a, theirs], rows_in.at[i, a, mine], y_send.at[s, a], y_recv.at[i], dev_j(other)
            ).start()
            return 0

        lax.fori_loop(1, 8, send, 0)

    def compute(c):
        base = pl.multiple_of(c * BATCH, 16)
        slots = (2 * c + 1, (2 * c + 2) % 8)
        for m, i in enumerate(slots):
            wait(rows_in.at[i, :, pl.ds(0, 7 * BLK)], y_recv.at[i])
            for a, store in ((0, xs), (1, ss)):
                flat = dot(perm[...], rows_in[i, a]).astype(BF16)
                for q in range(Q):
                    store[pl.ds(base + m * ROWS, ROWS), q * DQ : (q + 1) * DQ] = flat[
                        q * ROWS : (q + 1) * ROWS, :
                    ]
        batch = pl.ds(base, BATCH)
        x = xs[batch, :]
        pre_gate = dot(x, wg[...])
        pre_up = dot(x, wu[...])
        sig = jax.nn.sigmoid(pre_gate)
        hidden = (pre_gate * sig * pre_up).astype(BF16)
        grad_hidden = dot_nt(ss[batch, :], wd[...])
        grad_gate = (grad_hidden * pre_up * sig * (1.0 + pre_gate * (1.0 - sig))).astype(BF16)
        grad_up = (grad_hidden * pre_gate * sig).astype(BF16)
        hid[0, batch, :] = grad_gate
        hid[1, batch, :] = grad_up
        hid[2, batch, :] = hidden
        total = jnp.sum(grad_hidden * hidden.astype(F32), axis=1, keepdims=True)
        gs[batch, :] = jnp.broadcast_to(total, (BATCH, 128))
        out = dot(hidden, wd[...]).astype(BF16)
        for m, i in enumerate(slots):
            part = out[m * ROWS : (m + 1) * ROWS, :]
            flat = jnp.concatenate([part[:, q * DQ : (q + 1) * DQ] for q in range(Q)], axis=0)
            rows_in[i, 0] = dot(perm_t[...], flat).astype(BF16)
        grad = (dot_nt(grad_gate, wg[...]) + dot_nt(grad_up, wu[...])).astype(BF16)
        for m, i in enumerate(slots):
            part = grad[m * ROWS : (m + 1) * ROWS, :]
            flat = jnp.concatenate([part[:, q * DQ : (q + 1) * DQ] for q in range(Q)], axis=0)
            rows_in[i, 1] = dot(perm_t[...], flat).astype(BF16)

    def give_back(i):
        mine = pl.ds(pl.multiple_of(j * BLK, 16), BLK)
        for a in range(2):
            rows_back[i, a, mine, :] = rows_in[i, a, mine, :]

        def send(k, _):
            other = (j + k) % 8
            theirs = pl.ds(pl.multiple_of(other * BLK, 16), BLK)
            for a in range(2):
                remote(
                    rows_in.at[i, a, theirs], rows_back.at[i, a, mine], r_send.at[i], r_recv.at[i], dev_j(other)
                ).start()
            return 0

        lax.fori_loop(1, 8, send, 0)

    def group(g, _):
        first = jnp.minimum(jnp.maximum(2 * g - 1, 0), 8)
        last = jnp.minimum(2 * g + 1, 8)
        for a in range(2):

            def one(i, _, a=a):
                unit(i, a)
                return 0

            lax.fori_loop(first, last, one, 0)

        @pl.when(g == 2)
        def _():
            for copy in weights:
                copy.wait()

        @pl.when(g >= 2)
        def _():
            compute(g - 2)

        @pl.when(g == 4)
        def _():
            give_back(6)
            give_back(5)

        @pl.when(g == 5)
        def _():
            give_back(7)

        return 0

    lax.fori_loop(0, 6, group, 0)

    row = iota((8 * ROWS, 128), 0)
    lanes = iota((8 * ROWS, 128), 1)
    spread = jnp.where(lanes == row - div20(row) * CAP, gs[...], 0.0)
    row = iota((64, 8 * ROWS), 0)
    block = div20(iota((64, 8 * ROWS), 1))
    pick = jnp.where(row == (block & 7) * 8 + (((block >> 3) + 1) & 7), 1.0, 0.0)
    gp_a[...] = dot_f32(pick, spread)
    tile = pl.ds(pl.multiple_of(j * 8, 8), 8)
    gp_b[tile, :] = gp_a[tile, :]

    def send_gp(k, _):
        other = (j + k) % 8
        theirs = pl.ds(pl.multiple_of(other * 8, 8), 8)
        remote(gp_a.at[theirs], gp_b.at[tile], g_send.at[0], g_recv.at[0], dev_j(other)).start()
        return 0

    lax.fori_loop(1, 8, send_gp, 0)

    for s in range(4):
        for a in range(2):
            wait(sent.at[s, a, pl.ds(0, 7 * BLK)], y_send.at[s, a])

    def grads(n, _):
        for kind, store in ((0, xs), (1, xs), (2, ss)):
            cols = pl.ds(pl.multiple_of(n * DQ, 128), DQ)
            part = dot_tn(hid[kind], store[:, cols]).astype(BF16)
            if kind == 0:
                sent[n, 0, 0:F, :] = part
            elif kind == 1:
                sent[n, 1, 0:F, :] = part
            else:
                sent[n, 0, F:WROWS, :] = part[0 : F // 2, :]
                sent[n, 1, F:WROWS, :] = part[F // 2 :, :]
        return 0

    lax.fori_loop(0, 4, grads, 0)
    for k in range(1, 4):
        other = (mx + k) % 4
        remote(
            sent.at[other, :, pl.ds(0, WROWS)],
            wpart.at[k - 1],
            x_send.at[k - 1],
            x_recv.at[k - 1],
            dev_x(k),
        ).start()

    def back(t, _):
        i = 7 - t

        @pl.when(i >= 3)
        def _():
            give_back(i - 3)

        wait(rows_back.at[i, :, pl.ds(0, 7 * BLK)], r_recv.at[i])
        weighted = select(i, True)
        psum[0] = sum(dot_tn(m, rows_back[i, 0]) for m in weighted)
        psum[1] = dot_tn(select(i, False)[0], rows_back[i, 1])

        @pl.when((i >= 1) & (i <= 4))
        def _():
            wait(zback.at[i + 2], b_recv.at[i + 2])
            psum[...] = psum[...] + zback[i + 2].astype(F32)

        @pl.when(i == 5)
        def _():
            wait(zback.at[7, :, pl.ds(0, 256)], b_recv.at[0])
            psum[:, 0:256, :] = psum[:, 0:256, :] + zback[7, :, 0:256, :].astype(F32)

        @pl.when(i == 6)
        def _():
            wait(zback.at[7, :, pl.ds(256, 256)], b_recv.at[7])
            psum[:, 256:512, :] = psum[:, 256:512, :] + zback[7, :, 256:512, :].astype(F32)

        @pl.when((i >= 1) & (i <= 4))
        def _():
            wait(held.at[i], z_send.at[i])

        @pl.when((i >= 5) & (i <= 6))
        def _():
            wait(held.at[i, :, pl.ds(0, 256)], z_send.at[i])

        @pl.when(i >= 1)
        def _():
            held[i] = psum[...].astype(BF16)

        @pl.when((i >= 1) & (i <= 6))
        def _():
            step = 1 - 2 * (i % 2)
            remote(held.at[i], zback.at[i], b_send.at[i], b_recv.at[i], dev_z(step)).start()

        @pl.when(i == 7)
        def _():
            for lo, step, n in ((0, -1, 0), (256, 1, 7)):
                half = (7, slice(None), pl.ds(lo, 256))
                remote(held.at[half], zback.at[half], b_send.at[n], b_recv.at[n], dev_z(step)).start()

        @pl.when(i == 6)
        def _():
            wait(gp_b.at[pl.ds(0, 56)], g_recv.at[0])
            row = iota((64, 64), 0)
            col = iota((64, 64), 1)
            turn = jnp.where(col == (row & 7) * 8 + (row >> 3), 1.0, 0.0)
            gp_c[...] = dot_f32(turn, gp_b[...])
            own = pl.ds(pl.multiple_of(z * 8, 8), 8)
            gp_d[own, :] = gp_c[0:8, :]
            for i in range(1, 8):
                remote(
                    gp_c.at[pl.ds(i * 8, 8)], gp_d.at[own], g_send.at[1], g_recv.at[1], dev_z(offsets[i])
                ).start()

        @pl.when(i == 3)
        def _():
            wait(gp_d.at[pl.ds(0, 56)], g_recv.at[1])
            row = iota((64, T), 0)
            expert = (((row & 7) >> 1) << 4) + ((row >> 3) << 1) + (row & 1)
            code = jnp.concatenate([meta[p, 0:8, :] for p in range(NZ)], axis=0)
            dense = jnp.zeros((64, T), F32)
            values = gp_d[...]
            for n in range(CAP):
                dense = dense + jnp.where(code == float(n), values[:, n : n + 1], 0.0)
            for k in range(8):
                hit = routes_ref[k : k + 1, :] == expert
                found = jnp.sum(jnp.where(hit, dense, 0.0), axis=0, keepdims=True)
                gprob_ref[k : k + 1, :] = found / probs_ref[k : k + 1, :]

        @pl.when(i == 2)
        def _():
            for n in range(3):
                wait(wpart.at[n], x_recv.at[n])
            mine = sent[mx, :, 0:WROWS, :].astype(F32)
            total = ((mine + wpart[0].astype(F32)) + wpart[1].astype(F32)) + wpart[2].astype(F32)
            ogate_ref[...] = jnp.transpose(total[0, 0:F])
            oup_ref[...] = jnp.transpose(total[1, 0:F])
            odown_ref[0 : F // 2, :] = total[0, F:WROWS]
            odown_ref[F // 2 :, :] = total[1, F:WROWS]

        return 0

    lax.fori_loop(0, 8, back, 0)

    for n in (1, 2):
        wait(zback.at[n], b_recv.at[n])
    for a, ref in ((0, out_ref), (1, gtok_ref)):
        total = psum[a] + zback[1, a].astype(F32) + zback[2, a].astype(F32)
        for q in range(Q):
            ref[:, q * DQ : (q + 1) * DQ] = total[q * T : (q + 1) * T, :].astype(BF16)

    wait(held.at[pl.ds(0, 2)], z_send.at[0])
    for i in range(1, 8):
        wait(meta.at[0], m_send.at[i])
    for i in range(8):
        wait(rows_in.at[i, :, pl.ds(0, 7 * BLK)], r_send.at[i])
    for i in range(1, 7):
        wait(held.at[i], b_send.at[i])
    for lo, n in ((0, 0), (256, 7)):
        wait(held.at[7, :, pl.ds(lo, 256)], b_send.at[n])
    for n in range(3):
        wait(wpart.at[n], x_send.at[n])
    for n in range(2):
        wait(gp_b.at[pl.ds(0, 56)], g_send.at[n])


def shards(tokens, routes, gate_probs, cotangent, w_gate, w_up, w_down):
    vmem = pl.BlockSpec(memory_space=pltpu.VMEM)
    hbm = pl.BlockSpec(memory_space=pl.ANY)
    dma = pltpu.SemaphoreType.DMA
    out, gtok, gprob, ogate, oup, odown = pl.pallas_call(
        kernel,
        out_shape=(
            jax.ShapeDtypeStruct((T, D), BF16),
            jax.ShapeDtypeStruct((T, D), BF16),
            jax.ShapeDtypeStruct((8, T), F32),
            jax.ShapeDtypeStruct((F, F), F32),
            jax.ShapeDtypeStruct((F, F), F32),
            jax.ShapeDtypeStruct((F, F), F32),
        ),
        in_specs=[vmem] * 4 + [hbm] * 3,
        out_specs=(vmem,) * 6,
        scratch_shapes=[
            pltpu.VMEM((D, F), BF16),
            pltpu.VMEM((D, F), BF16),
            pltpu.VMEM((F, D), BF16),
            pltpu.VMEM((8, 2, TQ, DQ), BF16),
            pltpu.VMEM((4, 2, R, DQ), BF16),
            pltpu.VMEM((8, 2, R, DQ), BF16),
            pltpu.VMEM((8, 2, R, DQ), BF16),
            pltpu.VMEM((8 * ROWS, D), BF16),
            pltpu.VMEM((8 * ROWS, D), BF16),
            pltpu.VMEM((3, 8 * ROWS, F), BF16),
            pltpu.VMEM((8, 2, TQ, DQ), BF16),
            pltpu.VMEM((3, 2, WROWS, DQ), BF16),
            pltpu.VMEM((R, R), BF16),
            pltpu.VMEM((R, R), BF16),
            pltpu.VMEM((2, TQ, DQ), F32),
            pltpu.VMEM((8, 16, T), F32),
            pltpu.VMEM((8, 16, T), F32),
            pltpu.VMEM((8 * ROWS, 128), F32),
            pltpu.VMEM((64, 128), F32),
            pltpu.VMEM((64, 128), F32),
            pltpu.VMEM((64, 128), F32),
            pltpu.VMEM((64, 128), F32),
            dma((3,)),
            dma((7,)),
            dma((8, 2)),
            dma((8,)),
            dma((8,)),
            dma((4, 2)),
            dma((8,)),
            dma((8,)),
            dma((8,)),
            dma((8,)),
            dma((8,)),
            dma((3,)),
            dma((3,)),
            dma((2,)),
            dma((2,)),
        ],
        compiler_params=pltpu.CompilerParams(
            collective_id=0, has_side_effects=True, vmem_limit_bytes=63 * 2**20
        ),
        cost_estimate=pl.CostEstimate(flops=20 * 10**9, bytes_accessed=10**7, transcendentals=10**6),
    )(routes.T, gate_probs.T, tokens, cotangent, w_gate[0], w_up[0], w_down[0])
    return (out, gtok, gprob.T, ogate[None], oup[None], odown[None])


def solution(mesh):
    placed = (
        P(("mirror", "expert"), None),
        P(("mirror", "expert"), None),
        P(("mirror", "expert"), None),
        P(("mirror", "expert"), None),
        P("expert", None, None),
        P("expert", None, None),
        P("expert", None, None),
    )
    return jax.shard_map(
        shards,
        mesh=mesh,
        in_specs=placed,
        out_specs=(
            P(("mirror", "expert"), None),
            P(("mirror", "expert"), None),
            P(("mirror", "expert"), None),
            P("expert", "mirror", None),
            P("expert", "mirror", None),
            P("expert", None, "mirror"),
        ),
        check_vma=False,
    )
```

```python
import jax
import jax.numpy as jnp
from jax import lax
from jax.experimental import pallas as pl
from jax.experimental.pallas import tpu as pltpu
from jax.sharding import PartitionSpec as P

MESH = pl.DeviceIdType.MESH
F32 = jnp.float32
BF16 = jnp.bfloat16
NX, NY, NZ, NJ = 4, 4, 8, 8
T = 128
CAP = 20
Q = 4
DQ = 384
BLK = Q * CAP
R = NJ * BLK
TQ = Q * T
F = 384
D = 1536
ROWS = NJ * CAP
BATCH = 2 * ROWS
WROWS = F + F // 2


def dot(a, b):
    return jnp.dot(a, b, preferred_element_type=F32)


def dot_nt(a, b):
    return lax.dot_general(a, b, (((1,), (1,)), ((), ())), preferred_element_type=F32)


def dot_tn(a, b):
    return lax.dot_general(a, b, (((0,), (0,)), ((), ())), preferred_element_type=F32)


def dot_f32(a, b):
    return jnp.dot(a, b, preferred_element_type=F32, precision=lax.Precision.HIGHEST)


def iota(shape, dim):
    return lax.broadcasted_iota(jnp.int32, shape, dim)


def div20(v):
    return (v * 3277) >> 16


def wait(ref, sem):
    pltpu.make_async_copy(ref, ref, sem).wait()


def kernel(
    routes_ref, probs_ref, tok_ref, cot_ref, wg_hbm, wu_hbm, wd_hbm,
    out_ref, gtok_ref, gprob_ref, ogate_ref, oup_ref, odown_ref,
    wg, wu, wd, held, sent, rows_in, rows_back, xs, ss, hid, zback, wpart, perm, perm_t, psum,
    meta, meta_in, gs, gp_a, gp_b, gp_c, gp_d,
    w_sem, z_send, z_recv, m_send, m_recv, y_send, y_recv, r_send, r_recv,
    b_send, b_recv, x_send, x_recv, g_send, g_recv,
):
    mx = lax.axis_index("mirror")
    e = lax.axis_index("expert")
    y, z, core = e // 16, (e // 2) % 8, e % 2
    j = y * 2 + core

    def dev_j(other):
        return (mx, (other // 2) * 16 + z * 2 + other % 2)

    def dev_z(step):
        return (mx, y * 16 + ((z + step + 8) % 8) * 2 + core)

    def dev_x(step):
        return ((mx + step) % 4, e)

    offsets = [0, -1, 1, -2, 2, -3, 3, -4]

    barrier = pltpu.get_barrier_semaphore()
    for k in range(1, 8):
        pl.semaphore_signal(barrier, inc=1, device_id=dev_j((j + k) % 8), device_id_type=MESH)
        pl.semaphore_signal(barrier, inc=1, device_id=dev_z(k), device_id_type=MESH)
    for k in range(1, 4):
        pl.semaphore_signal(barrier, inc=1, device_id=dev_x(k), device_id_type=MESH)

    weights = [
        pltpu.make_async_copy(src, dst, w_sem.at[n])
        for n, (src, dst) in enumerate(((wg_hbm, wg), (wu_hbm, wu), (wd_hbm, wd)))
    ]
    for copy in weights:
        copy.start()

    for q in range(Q):
        held[0, 0, q * T : (q + 1) * T, :] = tok_ref[:, q * DQ : (q + 1) * DQ]
        held[0, 1, q * T : (q + 1) * T, :] = cot_ref[:, q * DQ : (q + 1) * DQ]

    row = iota((64, T), 0)
    expert = (((row & 7) >> 1) << 4) + ((row >> 3) << 1) + (row & 1)
    member = jnp.zeros((64, T), F32)
    weight = jnp.zeros((64, T), F32)
    for k in range(8):
        hit = routes_ref[k : k + 1, :] == expert
        member = member + jnp.where(hit, 1.0, 0.0)
        weight = weight + jnp.where(hit, probs_ref[k : k + 1, :], 0.0)
    before = jnp.where(iota((T, T), 0) < iota((T, T), 1), 1.0, 0.0).astype(BF16)
    rank = dot(member.astype(BF16), before)
    code = jnp.where(member > 0.5, rank, -1.0)
    for p in range(NZ):
        meta[p, 0:8, :] = code[p * 8 : (p + 1) * 8, :]
        meta[p, 8:16, :] = weight[p * 8 : (p + 1) * 8, :]
    meta_in[0] = meta[z]

    pl.semaphore_wait(barrier, 17)

    def remote(src, dst, send, recv, device):
        return pltpu.make_async_remote_copy(
            src_ref=src, dst_ref=dst, send_sem=send, recv_sem=recv, device_id=device, device_id_type=MESH
        )

    for a in range(2):
        for slot, step in ((1, 1), (2, -1)):
            remote(held.at[0, a], held.at[slot, a], z_send.at[0], z_recv.at[slot, a], dev_z(step)).start()
        if a == 0:
            for i in range(1, 8):
                to = -offsets[i]
                remote(
                    meta.at[(z + to + 8) % 8], meta_in.at[i], m_send.at[i], m_recv.at[i], dev_z(to)
                ).start()

    r80 = iota((BLK, T), 0)
    q80 = div20(r80)
    slot80 = (r80 - q80 * CAP).astype(F32)

    def select(i, weighted):
        tops, lows = [], []
        for n in range(NJ):
            hit = meta_in[i, n : n + 1, :] == slot80
            if weighted:
                value = jnp.where(hit, meta_in[i, 8 + n : 9 + n, :], 0.0)
            else:
                value = jnp.where(hit, 1.0, 0.0)
            parts = [jnp.where(q80 == q, value, 0.0) for q in range(Q)]
            block = jnp.concatenate(parts, axis=1)
            top = block.astype(BF16)
            tops.append(top)
            if weighted:
                lows.append((block - top.astype(F32)).astype(BF16))
        top = jnp.concatenate(tops, axis=0)
        return (top, jnp.concatenate(lows, axis=0)) if weighted else (top,)

    def unit(i, a):
        s = i % 4

        @pl.when(i >= 1)
        def _():
            wait(held.at[i, a], z_recv.at[i, a])

        @pl.when((i >= 1) & (i <= 4))
        def _():
            step = 2 * (i % 2) - 1
            remote(held.at[i, a], held.at[i + 2, a], z_send.at[i], z_recv.at[i + 2, a], dev_z(step)).start()

        @pl.when(i == 5)
        def _():
            half = held.at[5, a, pl.ds(0, 256)]
            remote(half, held.at[7, a, pl.ds(0, 256)], z_send.at[5], z_recv.at[7, a], dev_z(1)).start()

        @pl.when(i == 6)
        def _():
            half = held.at[6, a, pl.ds(256, 256)]
            remote(half, held.at[7, a, pl.ds(256, 256)], z_send.at[6], z_recv.at[7, a], dev_z(-1)).start()

        if a == 0:

            @pl.when(i >= 1)
            def _():
                wait(meta_in.at[i], m_recv.at[i])

        source = held[i, a]
        picked = sum(dot(m, source) for m in select(i, a == 1))

        @pl.when(i >= 4)
        def _():
            wait(sent.at[s, a, pl.ds(0, 7 * BLK)], y_send.at[s, a])

        sent[s, a] = picked.astype(BF16)
        mine = pl.ds(pl.multiple_of(j * BLK, 16), BLK)
        rows_in[i, a, mine, :] = sent[s, a, mine, :]

        def send(k, _):
            other = (j + k) % 8
            theirs = pl.ds(pl.multiple_of(other * BLK, 16), BLK)
            remote(
                sent.at[s, a, theirs], rows_in.at[i, a, mine], y_send.at[s, a], y_recv.at[i], dev_j(other)
            ).start()
            return 0

        lax.fori_loop(1, 8, send, 0)

    def compute(c):
        base = pl.multiple_of(c * BATCH, 16)
        slots = (2 * c + 1, (2 * c + 2) % 8)
        for m, i in enumerate(slots):
            wait(rows_in.at[i, :, pl.ds(0, 7 * BLK)], y_recv.at[i])
            for a, store in ((0, xs), (1, ss)):
                flat = dot(perm[...], rows_in[i, a]).astype(BF16)
                for q in range(Q):
                    store[pl.ds(base + m * ROWS, ROWS), q * DQ : (q + 1) * DQ] = flat[
                        q * ROWS : (q + 1) * ROWS, :
                    ]
        batch = pl.ds(base, BATCH)
        x = xs[batch, :]
        pre_gate = dot(x, wg[...])
        pre_up = dot(x, wu[...])
        sig = jax.nn.sigmoid(pre_gate)
        hidden = (pre_gate * sig * pre_up).astype(BF16)
        grad_hidden = dot_nt(ss[batch, :], wd[...])
        grad_gate = (grad_hidden * pre_up * sig * (1.0 + pre_gate * (1.0 - sig))).astype(BF16)
        grad_up = (grad_hidden * pre_gate * sig).astype(BF16)
        hid[0, batch, :] = grad_gate
        hid[1, batch, :] = grad_up
        hid[2, batch, :] = hidden
        total = jnp.sum(grad_hidden * hidden.astype(F32), axis=1, keepdims=True)
        gs[batch, :] = jnp.broadcast_to(total, (BATCH, 128))
        out = dot(hidden, wd[...]).astype(BF16)
        for m, i in enumerate(slots):
            part = out[m * ROWS : (m + 1) * ROWS, :]
            flat = jnp.concatenate([part[:, q * DQ : (q + 1) * DQ] for q in range(Q)], axis=0)
            rows_in[i, 0] = dot(perm_t[...], flat).astype(BF16)
        grad = (dot_nt(grad_gate, wg[...]) + dot_nt(grad_up, wu[...])).astype(BF16)
        for m, i in enumerate(slots):
            part = grad[m * ROWS : (m + 1) * ROWS, :]
            flat = jnp.concatenate([part[:, q * DQ : (q + 1) * DQ] for q in range(Q)], axis=0)
            rows_in[i, 1] = dot(perm_t[...], flat).astype(BF16)

    def give_back(i, a):
        mine = pl.ds(pl.multiple_of(j * BLK, 16), BLK)
        rows_back[i, a, mine, :] = rows_in[i, a, mine, :]

        def send(k, _):
            other = (j + k) % 8
            theirs = pl.ds(pl.multiple_of(other * BLK, 16), BLK)
            remote(
                rows_in.at[i, a, theirs], rows_back.at[i, a, mine], r_send.at[i], r_recv.at[i, a], dev_j(other)
            ).start()
            return 0

        lax.fori_loop(1, 8, send, 0)

    def give_group(g):
        first, last = bounds(g)
        for a in range(2):

            def one(i, _, a=a):
                give_back(i, a)
                return 0

            lax.fori_loop(first, last, one, 0)

    def bounds(g):
        return jnp.minimum(jnp.maximum(2 * g - 1, 0), 8), jnp.minimum(2 * g + 1, 8)

    def make_perms():
        lane = iota((R, R), 1)
        r = iota((R, R), 0)
        r20 = div20(r)
        slot_of = r - r20 * 20
        perm[...] = jnp.where(lane == (r20 & 7) * BLK + (r20 >> 3) * CAP + slot_of, 1.0, 0.0).astype(BF16)
        perm_t[...] = jnp.where(
            lane == (r20 & 3) * ROWS + (r20 >> 2) * CAP + slot_of, 1.0, 0.0
        ).astype(BF16)


    def group(g, _):
        first, last = bounds(g)
        for a in range(2):

            def one(i, _, a=a):
                unit(i, a)
                return 0

            lax.fori_loop(first, last, one, 0)

        @pl.when(g == 0)
        def _():
            make_perms()

        @pl.when(g == 2)
        def _():
            for copy in weights:
                copy.wait()

        @pl.when(g >= 2)
        def _():
            compute(g - 2)

        @pl.when(g == 4)
        def _():
            for a in range(2):
                give_back(6, a)

        @pl.when(g == 5)
        def _():
            for i in (7, 5):
                for a in range(2):
                    give_back(i, a)

        return 0

    lax.fori_loop(0, 6, group, 0)

    row = iota((8 * ROWS, 128), 0)
    lanes = iota((8 * ROWS, 128), 1)
    spread = jnp.where(lanes == row - div20(row) * CAP, gs[...], 0.0)
    row = iota((64, 8 * ROWS), 0)
    block = div20(iota((64, 8 * ROWS), 1))
    pick = jnp.where(row == (block & 7) * 8 + (((block >> 3) + 1) & 7), 1.0, 0.0)
    gp_a[...] = dot_f32(pick, spread)
    tile = pl.ds(pl.multiple_of(j * 8, 8), 8)
    gp_b[tile, :] = gp_a[tile, :]

    def send_gp(k, _):
        other = (j + k) % 8
        theirs = pl.ds(pl.multiple_of(other * 8, 8), 8)
        remote(gp_a.at[theirs], gp_b.at[tile], g_send.at[0], g_recv.at[0], dev_j(other)).start()
        return 0

    lax.fori_loop(1, 8, send_gp, 0)

    for s in range(4):
        for a in range(2):
            wait(sent.at[s, a, pl.ds(0, 7 * BLK)], y_send.at[s, a])

    def grads(n, _):
        for kind, store in ((0, xs), (1, xs), (2, ss)):
            cols = pl.ds(pl.multiple_of(n * DQ, 128), DQ)
            part = dot_tn(hid[kind], store[:, cols]).astype(BF16)
            if kind == 0:
                sent[n, 0, 0:F, :] = part
            elif kind == 1:
                sent[n, 1, 0:F, :] = part
            else:
                sent[n, 0, F:WROWS, :] = part[0 : F // 2, :]
                sent[n, 1, F:WROWS, :] = part[F // 2 :, :]
        return 0

    lax.fori_loop(0, 4, grads, 0)
    for k in range(1, 4):
        other = (mx + k) % 4
        remote(
            sent.at[other, :, pl.ds(0, WROWS)],
            wpart.at[k - 1],
            x_send.at[k - 1],
            x_recv.at[k - 1],
            dev_x(k),
        ).start()

    def back_unit(i, a):
        wait(rows_back.at[i, a, pl.ds(0, 7 * BLK)], r_recv.at[i, a])
        psum[a] = sum(dot_tn(m, rows_back[i, a]) for m in select(i, a == 0))

        @pl.when((i >= 1) & (i <= 4))
        def _():
            wait(zback.at[i + 2, a], b_recv.at[i + 2, a])
            psum[a] = psum[a] + zback[i + 2, a].astype(F32)

        @pl.when(i == 5)
        def _():
            wait(zback.at[7, a, pl.ds(0, 256)], b_recv.at[0, a])
            psum[a, 0:256, :] = psum[a, 0:256, :] + zback[7, a, 0:256, :].astype(F32)

        @pl.when(i == 6)
        def _():
            wait(zback.at[7, a, pl.ds(256, 256)], b_recv.at[7, a])
            psum[a, 256:512, :] = psum[a, 256:512, :] + zback[7, a, 256:512, :].astype(F32)

        if a == 0:

            @pl.when((i >= 1) & (i <= 4))
            def _():
                wait(held.at[i], z_send.at[i])

            @pl.when((i >= 5) & (i <= 6))
            def _():
                wait(held.at[i, :, pl.ds(0, 256)], z_send.at[i])

        @pl.when(i >= 1)
        def _():
            held[i, a] = psum[a].astype(BF16)

        @pl.when((i >= 1) & (i <= 6))
        def _():
            step = 1 - 2 * (i % 2)
            remote(held.at[i, a], zback.at[i, a], b_send.at[i], b_recv.at[i, a], dev_z(step)).start()

        @pl.when(i == 7)
        def _():
            for lo, step, n in ((0, -1, 0), (256, 1, 7)):
                half = (7, a, pl.ds(lo, 256))
                remote(held.at[half], zback.at[half], b_send.at[n], b_recv.at[n, a], dev_z(step)).start()

    def back(t, _):
        g = 4 - t
        first, last = bounds(g)

        @pl.when((g >= 1) & (g <= 3))
        def _():
            give_group(g - 1)

        for a in range(2):

            def one(i, _, a=a):
                back_unit(i, a)
                return 0

            lax.fori_loop(first, last, one, 0)

        @pl.when(g == 3)
        def _():
            wait(gp_b.at[pl.ds(0, 56)], g_recv.at[0])
            row = iota((64, 64), 0)
            col = iota((64, 64), 1)
            turn = jnp.where(col == (row & 7) * 8 + (row >> 3), 1.0, 0.0)
            gp_c[...] = dot_f32(turn, gp_b[...])
            own = pl.ds(pl.multiple_of(z * 8, 8), 8)
            gp_d[own, :] = gp_c[0:8, :]
            for i in range(1, 8):
                remote(
                    gp_c.at[pl.ds(i * 8, 8)], gp_d.at[own], g_send.at[1], g_recv.at[1], dev_z(offsets[i])
                ).start()

        @pl.when(g == 2)
        def _():
            wait(gp_d.at[pl.ds(0, 56)], g_recv.at[1])
            row = iota((64, T), 0)
            expert = (((row & 7) >> 1) << 4) + ((row >> 3) << 1) + (row & 1)
            code = jnp.concatenate([meta[p, 0:8, :] for p in range(NZ)], axis=0)
            dense = jnp.zeros((64, T), F32)
            values = gp_d[...]
            for n in range(CAP):
                dense = dense + jnp.where(code == float(n), values[:, n : n + 1], 0.0)
            for k in range(8):
                hit = routes_ref[k : k + 1, :] == expert
                found = jnp.sum(jnp.where(hit, dense, 0.0), axis=0, keepdims=True)
                gprob_ref[k : k + 1, :] = found / probs_ref[k : k + 1, :]

        @pl.when(g == 1)
        def _():
            for n in range(3):
                wait(wpart.at[n], x_recv.at[n])
            mine = sent[mx, :, 0:WROWS, :].astype(F32)
            total = ((mine + wpart[0].astype(F32)) + wpart[1].astype(F32)) + wpart[2].astype(F32)
            ogate_ref[...] = jnp.transpose(total[0, 0:F])
            oup_ref[...] = jnp.transpose(total[1, 0:F])
            odown_ref[0 : F // 2, :] = total[0, F:WROWS]
            odown_ref[F // 2 :, :] = total[1, F:WROWS]

        return 0

    lax.fori_loop(0, 5, back, 0)

    for a, ref in ((0, out_ref), (1, gtok_ref)):
        for n in (1, 2):
            wait(zback.at[n, a], b_recv.at[n, a])
        total = psum[a] + zback[1, a].astype(F32) + zback[2, a].astype(F32)
        for q in range(Q):
            ref[:, q * DQ : (q + 1) * DQ] = total[q * T : (q + 1) * T, :].astype(BF16)

    wait(held.at[pl.ds(0, 2)], z_send.at[0])
    for i in range(1, 8):
        wait(meta.at[0], m_send.at[i])
    for i in range(8):
        wait(rows_in.at[i, :, pl.ds(0, 7 * BLK)], r_send.at[i])
    for i in range(1, 7):
        wait(held.at[i], b_send.at[i])
    for lo, n in ((0, 0), (256, 7)):
        wait(held.at[7, :, pl.ds(lo, 256)], b_send.at[n])
    for n in range(3):
        wait(wpart.at[n], x_send.at[n])
    for n in range(2):
        wait(gp_b.at[pl.ds(0, 56)], g_send.at[n])


def place(*refs):
    stage, sems = refs[12:18], refs[18]
    loads = [pltpu.make_async_copy(refs[n], stage[n], sems.at[0, n]) for n in range(6)]
    stores = [pltpu.make_async_copy(stage[n], refs[n + 6], sems.at[1, n]) for n in range(6)]
    for copy in loads:
        copy.start()
    for load, store in zip(loads, stores):
        load.wait()
        store.start()
    for copy in stores:
        copy.wait()


def shards(tokens, routes, gate_probs, cotangent, w_gate, w_up, w_down):
    vmem = pl.BlockSpec(memory_space=pltpu.VMEM)
    hbm = pl.BlockSpec(memory_space=pl.ANY)
    dma = pltpu.SemaphoreType.DMA
    results = pl.pallas_call(
        kernel,
        out_shape=(
            jax.ShapeDtypeStruct((T, D), BF16),
            jax.ShapeDtypeStruct((T, D), BF16),
            jax.ShapeDtypeStruct((8, T), F32),
            jax.ShapeDtypeStruct((F, F), F32),
            jax.ShapeDtypeStruct((F, F), F32),
            jax.ShapeDtypeStruct((F, F), F32),
        ),
        in_specs=[vmem] * 4 + [hbm] * 3,
        out_specs=(vmem,) * 6,
        scratch_shapes=[
            pltpu.VMEM((D, F), BF16),
            pltpu.VMEM((D, F), BF16),
            pltpu.VMEM((F, D), BF16),
            pltpu.VMEM((8, 2, TQ, DQ), BF16),
            pltpu.VMEM((4, 2, R, DQ), BF16),
            pltpu.VMEM((8, 2, R, DQ), BF16),
            pltpu.VMEM((8, 2, R, DQ), BF16),
            pltpu.VMEM((8 * ROWS, D), BF16),
            pltpu.VMEM((8 * ROWS, D), BF16),
            pltpu.VMEM((3, 8 * ROWS, F), BF16),
            pltpu.VMEM((8, 2, TQ, DQ), BF16),
            pltpu.VMEM((3, 2, WROWS, DQ), BF16),
            pltpu.VMEM((R, R), BF16),
            pltpu.VMEM((R, R), BF16),
            pltpu.VMEM((2, TQ, DQ), F32),
            pltpu.VMEM((8, 16, T), F32),
            pltpu.VMEM((8, 16, T), F32),
            pltpu.VMEM((8 * ROWS, 128), F32),
            pltpu.VMEM((64, 128), F32),
            pltpu.VMEM((64, 128), F32),
            pltpu.VMEM((64, 128), F32),
            pltpu.VMEM((64, 128), F32),
            dma((3,)),
            dma((7,)),
            dma((8, 2)),
            dma((8,)),
            dma((8,)),
            dma((4, 2)),
            dma((8,)),
            dma((8,)),
            dma((8, 2)),
            dma((8,)),
            dma((8, 2)),
            dma((3,)),
            dma((3,)),
            dma((2,)),
            dma((2,)),
        ],
        compiler_params=pltpu.CompilerParams(
            collective_id=0, has_side_effects=True, vmem_limit_bytes=63 * 2**20
        ),
        cost_estimate=pl.CostEstimate(flops=20 * 10**9, bytes_accessed=10**7, transcendentals=10**6),
    )(routes.T, gate_probs.T, tokens, cotangent, w_gate[0], w_up[0], w_down[0])
    out, gtok, gprob, ogate, oup, odown = pl.pallas_call(
        place,
        out_shape=tuple(jax.ShapeDtypeStruct(v.shape, v.dtype) for v in results),
        in_specs=[hbm] * 6,
        out_specs=(hbm,) * 6,
        scratch_shapes=[pltpu.VMEM(v.shape, v.dtype) for v in results] + [dma((2, 6))],
    )(*results)
    return (out, gtok, gprob.T, ogate[None], oup[None], odown[None])


def solution(mesh):
    placed = (
        P(("mirror", "expert"), None),
        P(("mirror", "expert"), None),
        P(("mirror", "expert"), None),
        P(("mirror", "expert"), None),
        P("expert", None, None),
        P("expert", None, None),
        P("expert", None, None),
    )
    return jax.shard_map(
        shards,
        mesh=mesh,
        in_specs=placed,
        out_specs=(
            P(("mirror", "expert"), None),
            P(("mirror", "expert"), None),
            P(("mirror", "expert"), None),
            P("expert", "mirror", None),
            P("expert", "mirror", None),
            P("expert", None, "mirror"),
        ),
        check_vma=False,
    )
```

```python
import jax
import jax.numpy as jnp
from jax import lax
from jax.experimental import pallas as pl
from jax.experimental.pallas import tpu as pltpu
from jax.sharding import PartitionSpec as P

MESH = pl.DeviceIdType.MESH
F32 = jnp.float32
BF16 = jnp.bfloat16
NX, NY, NZ, NJ = 4, 4, 8, 8
T = 128
CAP = 20
Q = 4
DQ = 384
BLK = Q * CAP
R = NJ * BLK
TQ = Q * T
F = 384
D = 1536
ROWS = NJ * CAP
BATCH = 2 * ROWS
WROWS = F + F // 2


def dot(a, b):
    return jnp.dot(a, b, preferred_element_type=F32)


def dot_nt(a, b):
    return lax.dot_general(a, b, (((1,), (1,)), ((), ())), preferred_element_type=F32)


def dot_tn(a, b):
    return lax.dot_general(a, b, (((0,), (0,)), ((), ())), preferred_element_type=F32)


def dot_f32(a, b):
    return jnp.dot(a, b, preferred_element_type=F32, precision=lax.Precision.HIGHEST)


def iota(shape, dim):
    return lax.broadcasted_iota(jnp.int32, shape, dim)


def div20(v):
    return (v * 3277) >> 16


def wait(ref, sem):
    pltpu.make_async_copy(ref, ref, sem).wait()


def kernel(
    routes_ref, probs_ref, tok_hbm, cot_hbm, wg_hbm, wu_hbm, wd_hbm,
    out_ref, gtok_ref, gprob_ref, ogate_ref, oup_ref, odown_ref,
    wg, wu, wd, held, sent, rows_in, rows_back, xs, ss, hid, zback, wpart, perm, perm_t, psum,
    meta, meta_in, gs, gp_a, gp_b, gp_c, gp_d,
    t_sem, w_sem, z_send, z_recv, m_send, m_recv, y_send, y_recv, r_send, r_recv,
    b_send, b_recv, x_send, x_recv, g_send, g_recv,
):
    mx = lax.axis_index("mirror")
    e = lax.axis_index("expert")
    y, z, core = e // 16, (e // 2) % 8, e % 2
    j = y * 2 + core

    def dev_j(other):
        return (mx, (other // 2) * 16 + z * 2 + other % 2)

    def dev_z(step):
        return (mx, y * 16 + ((z + step + 8) % 8) * 2 + core)

    def dev_x(step):
        return ((mx + step) % 4, e)

    offsets = [0, -1, 1, -2, 2, -3, 3, -4]

    barrier = pltpu.get_barrier_semaphore()
    for k in range(1, 8):
        pl.semaphore_signal(barrier, inc=1, device_id=dev_j((j + k) % 8), device_id_type=MESH)
        pl.semaphore_signal(barrier, inc=1, device_id=dev_z(k), device_id_type=MESH)
    for k in range(1, 4):
        pl.semaphore_signal(barrier, inc=1, device_id=dev_x(k), device_id_type=MESH)

    own = [
        pltpu.make_async_copy(src.at[:, pl.ds(q * DQ, DQ)], held.at[0, a, pl.ds(q * T, T)], t_sem.at[a, q])
        for a, src in enumerate((tok_hbm, cot_hbm))
        for q in range(Q)
    ]
    for copy in own:
        copy.start()

    weights = [
        pltpu.make_async_copy(src, dst, w_sem.at[n])
        for n, (src, dst) in enumerate(((wg_hbm, wg), (wu_hbm, wu), (wd_hbm, wd)))
    ]
    for copy in weights:
        copy.start()

    row = iota((64, T), 0)
    expert = (((row & 7) >> 1) << 4) + ((row >> 3) << 1) + (row & 1)
    member = jnp.zeros((64, T), F32)
    weight = jnp.zeros((64, T), F32)
    for k in range(8):
        hit = routes_ref[k : k + 1, :] == expert
        member = member + jnp.where(hit, 1.0, 0.0)
        weight = weight + jnp.where(hit, probs_ref[k : k + 1, :], 0.0)
    before = jnp.where(iota((T, T), 0) < iota((T, T), 1), 1.0, 0.0).astype(BF16)
    rank = dot(member.astype(BF16), before)
    code = jnp.where(member > 0.5, rank, -1.0)
    for p in range(NZ):
        meta[p, 0:8, :] = code[p * 8 : (p + 1) * 8, :]
        meta[p, 8:16, :] = weight[p * 8 : (p + 1) * 8, :]
    meta_in[0] = meta[z]

    def remote(src, dst, send, recv, device):
        return pltpu.make_async_remote_copy(
            src_ref=src, dst_ref=dst, send_sem=send, recv_sem=recv, device_id=device, device_id_type=MESH
        )

    r80 = iota((BLK, T), 0)
    q80 = div20(r80)
    slot80 = (r80 - q80 * CAP).astype(F32)

    def select(i, weighted):
        tops, lows = [], []
        for n in range(NJ):
            hit = meta_in[i, n : n + 1, :] == slot80
            if weighted:
                value = jnp.where(hit, meta_in[i, 8 + n : 9 + n, :], 0.0)
            else:
                value = jnp.where(hit, 1.0, 0.0)
            parts = [jnp.where(q80 == q, value, 0.0) for q in range(Q)]
            block = jnp.concatenate(parts, axis=1)
            top = block.astype(BF16)
            tops.append(top)
            if weighted:
                lows.append((block - top.astype(F32)).astype(BF16))
        top = jnp.concatenate(tops, axis=0)
        return (top, jnp.concatenate(lows, axis=0)) if weighted else (top,)

    def unit(i, a):
        s = i % 4
        wait(held.at[i, a], z_recv.at[i, a])

        @pl.when((i >= 1) & (i <= 4))
        def _():
            step = 2 * (i % 2) - 1
            remote(held.at[i, a], held.at[i + 2, a], z_send.at[i], z_recv.at[i + 2, a], dev_z(step)).start()

        @pl.when(i == 5)
        def _():
            half = held.at[5, a, pl.ds(0, 256)]
            remote(half, held.at[7, a, pl.ds(0, 256)], z_send.at[5], z_recv.at[7, a], dev_z(1)).start()

        @pl.when(i == 6)
        def _():
            half = held.at[6, a, pl.ds(256, 256)]
            remote(half, held.at[7, a, pl.ds(256, 256)], z_send.at[6], z_recv.at[7, a], dev_z(-1)).start()

        if a == 0:

            wait(meta_in.at[i], m_recv.at[i])

        @pl.when(i >= 4)
        def _():
            wait(sent.at[s, a, pl.ds(0, 7 * BLK)], y_send.at[s, a])

        pick(i, a)
        send_out(i, a)

    def pick(i, a):
        s = i % 4
        source = held[i, a]
        picked = sum(dot(m, source) for m in select(i, a == 1))
        sent[s, a] = picked.astype(BF16)
        mine = pl.ds(pl.multiple_of(j * BLK, 16), BLK)
        rows_in[i, a, mine, :] = sent[s, a, mine, :]

    def send_out(i, a):
        s = i % 4
        mine = pl.ds(pl.multiple_of(j * BLK, 16), BLK)

        def send(k, _):
            other = (j + k) % 8
            theirs = pl.ds(pl.multiple_of(other * BLK, 16), BLK)
            remote(
                sent.at[s, a, theirs], rows_in.at[i, a, mine], y_send.at[s, a], y_recv.at[i], dev_j(other)
            ).start()
            return 0

        lax.fori_loop(1, 8, send, 0)

    def compute(c):
        base = pl.multiple_of(c * BATCH, 16)
        slots = (2 * c + 1, (2 * c + 2) % 8)
        for m, i in enumerate(slots):
            wait(rows_in.at[i, :, pl.ds(0, 7 * BLK)], y_recv.at[i])
            for a, store in ((0, xs), (1, ss)):
                flat = dot(perm[...], rows_in[i, a]).astype(BF16)
                for q in range(Q):
                    store[pl.ds(base + m * ROWS, ROWS), q * DQ : (q + 1) * DQ] = flat[
                        q * ROWS : (q + 1) * ROWS, :
                    ]
        batch = pl.ds(base, BATCH)
        x = xs[batch, :]
        pre_gate = dot(x, wg[...])
        pre_up = dot(x, wu[...])
        sig = jax.nn.sigmoid(pre_gate)
        hidden = (pre_gate * sig * pre_up).astype(BF16)
        grad_hidden = dot_nt(ss[batch, :], wd[...])
        grad_gate = (grad_hidden * pre_up * sig * (1.0 + pre_gate * (1.0 - sig))).astype(BF16)
        grad_up = (grad_hidden * pre_gate * sig).astype(BF16)
        hid[0, batch, :] = grad_gate
        hid[1, batch, :] = grad_up
        hid[2, batch, :] = hidden
        total = jnp.sum(grad_hidden * hidden.astype(F32), axis=1, keepdims=True)
        gs[batch, :] = jnp.broadcast_to(total, (BATCH, 128))
        out = dot(hidden, wd[...]).astype(BF16)
        for m, i in enumerate(slots):
            part = out[m * ROWS : (m + 1) * ROWS, :]
            flat = jnp.concatenate([part[:, q * DQ : (q + 1) * DQ] for q in range(Q)], axis=0)
            rows_in[i, 0] = dot(perm_t[...], flat).astype(BF16)
        grad = (dot_nt(grad_gate, wg[...]) + dot_nt(grad_up, wu[...])).astype(BF16)
        for m, i in enumerate(slots):
            part = grad[m * ROWS : (m + 1) * ROWS, :]
            flat = jnp.concatenate([part[:, q * DQ : (q + 1) * DQ] for q in range(Q)], axis=0)
            rows_in[i, 1] = dot(perm_t[...], flat).astype(BF16)

    def give_back(i, a):
        mine = pl.ds(pl.multiple_of(j * BLK, 16), BLK)
        rows_back[i, a, mine, :] = rows_in[i, a, mine, :]

        def send(k, _):
            other = (j + k) % 8
            theirs = pl.ds(pl.multiple_of(other * BLK, 16), BLK)
            remote(
                rows_in.at[i, a, theirs], rows_back.at[i, a, mine], r_send.at[i], r_recv.at[i, a], dev_j(other)
            ).start()
            return 0

        lax.fori_loop(1, 8, send, 0)

    def give(slots, a):
        def one(n, _):
            give_back(slots - n, a)
            return 0

        return one

    def bounds(g):
        return jnp.minimum(jnp.maximum(2 * g - 1, 0), 8), jnp.minimum(2 * g + 1, 8)

    def make_perms():
        lane = iota((R, R), 1)
        r = iota((R, R), 0)
        r20 = div20(r)
        slot_of = r - r20 * 20
        perm[...] = jnp.where(lane == (r20 & 7) * BLK + (r20 >> 3) * CAP + slot_of, 1.0, 0.0).astype(BF16)
        perm_t[...] = jnp.where(
            lane == (r20 & 3) * ROWS + (r20 >> 2) * CAP + slot_of, 1.0, 0.0
        ).astype(BF16)


    def group(g, _):
        first, last = bounds(g)
        for a in range(2):

            def one(i, _, a=a):
                unit(i, a)
                return 0

            lax.fori_loop(first, last, one, 0)

        @pl.when(g == 2)
        def _():
            for copy in weights:
                copy.wait()

        @pl.when(g >= 2)
        def _():
            compute(g - 2)

        @pl.when(g == 4)
        def _():
            for a in range(2):
                give_back(6, a)

        @pl.when(g == 5)
        def _():
            for i in (7, 5):
                for a in range(2):
                    give_back(i, a)

        return 0

    for a in range(2):
        for copy in own[a * Q : (a + 1) * Q]:
            copy.wait()
        pick(0, a)
    pl.semaphore_wait(barrier, 17)
    send_out(0, 0)
    for a in range(2):
        for slot, step in ((1, 1), (2, -1)):
            remote(held.at[0, a], held.at[slot, a], z_send.at[0], z_recv.at[slot, a], dev_z(step)).start()
        if a == 0:
            for i in range(1, 8):
                to = -offsets[i]
                remote(
                    meta.at[(z + to + 8) % 8], meta_in.at[i], m_send.at[i], m_recv.at[i], dev_z(to)
                ).start()
    send_out(0, 1)
    make_perms()
    lax.fori_loop(1, 6, group, 0)

    row = iota((8 * ROWS, 128), 0)
    lanes = iota((8 * ROWS, 128), 1)
    spread = jnp.where(lanes == row - div20(row) * CAP, gs[...], 0.0)
    row = iota((64, 8 * ROWS), 0)
    block = div20(iota((64, 8 * ROWS), 1))
    pick = jnp.where(row == (block & 7) * 8 + (((block >> 3) + 1) & 7), 1.0, 0.0)
    gp_a[...] = dot_f32(pick, spread)
    tile = pl.ds(pl.multiple_of(j * 8, 8), 8)
    gp_b[tile, :] = gp_a[tile, :]

    def send_gp(k, _):
        other = (j + k) % 8
        theirs = pl.ds(pl.multiple_of(other * 8, 8), 8)
        remote(gp_a.at[theirs], gp_b.at[tile], g_send.at[0], g_recv.at[0], dev_j(other)).start()
        return 0

    lax.fori_loop(1, 8, send_gp, 0)

    for s in range(4):
        for a in range(2):
            wait(sent.at[s, a, pl.ds(0, 7 * BLK)], y_send.at[s, a])

    def grads(n, _):
        for kind, store in ((0, xs), (1, xs), (2, ss)):
            cols = pl.ds(pl.multiple_of(n * DQ, 128), DQ)
            part = dot_tn(hid[kind], store[:, cols]).astype(BF16)
            if kind == 0:
                sent[n, 0, 0:F, :] = part
            elif kind == 1:
                sent[n, 1, 0:F, :] = part
            else:
                sent[n, 0, F:WROWS, :] = part[0 : F // 2, :]
                sent[n, 1, F:WROWS, :] = part[F // 2 :, :]
        return 0

    lax.fori_loop(0, 4, grads, 0)
    for k in range(1, 4):
        other = (mx + k) % 4
        remote(
            sent.at[other, :, pl.ds(0, WROWS)],
            wpart.at[k - 1],
            x_send.at[k - 1],
            x_recv.at[k - 1],
            dev_x(k),
        ).start()

    def back_unit(i, a):
        wait(rows_back.at[i, a, pl.ds(0, 7 * BLK)], r_recv.at[i, a])
        psum[a] = sum(dot_tn(m, rows_back[i, a]) for m in select(i, a == 0))

        @pl.when((i >= 1) & (i <= 4))
        def _():
            wait(zback.at[i + 2, a], b_recv.at[i + 2, a])
            psum[a] = psum[a] + zback[i + 2, a].astype(F32)

        @pl.when(i == 5)
        def _():
            wait(zback.at[7, a, pl.ds(0, 256)], b_recv.at[0, a])
            psum[a, 0:256, :] = psum[a, 0:256, :] + zback[7, a, 0:256, :].astype(F32)

        @pl.when(i == 6)
        def _():
            wait(zback.at[7, a, pl.ds(256, 256)], b_recv.at[7, a])
            psum[a, 256:512, :] = psum[a, 256:512, :] + zback[7, a, 256:512, :].astype(F32)

        if a == 0:

            @pl.when((i >= 1) & (i <= 4))
            def _():
                wait(held.at[i], z_send.at[i])

            @pl.when((i >= 5) & (i <= 6))
            def _():
                wait(held.at[i, :, pl.ds(0, 256)], z_send.at[i])

        @pl.when(i >= 1)
        def _():
            held[i, a] = psum[a].astype(BF16)

        @pl.when((i >= 1) & (i <= 6))
        def _():
            step = 1 - 2 * (i % 2)
            remote(held.at[i, a], zback.at[i, a], b_send.at[i], b_recv.at[i, a], dev_z(step)).start()

        @pl.when(i == 7)
        def _():
            for lo, step, n in ((0, -1, 0), (256, 1, 7)):
                half = (7, a, pl.ds(lo, 256))
                remote(held.at[half], zback.at[half], b_send.at[n], b_recv.at[n, a], dev_z(step)).start()

    def back(t, _):
        first = jnp.where(t == 0, 7, jnp.where(t == 1, 6, jnp.where(t == 4, 0, 4)))
        plain = jnp.where(t == 1, 2, 1)

        @pl.when(t == 1)
        def _():
            lax.fori_loop(0, 4, give(4, 0), 0)

        @pl.when(t == 2)
        def _():
            lax.fori_loop(0, 4, give(4, 1), 0)

        @pl.when(t == 3)
        def _():
            for a in range(2):
                give_back(0, a)

        for a in range(2):
            count = jnp.where(t == 2 + a, 4, jnp.where(t == 3 - a, 0, plain))

            def one(n, _, a=a):
                back_unit(first - n, a)
                return 0

            lax.fori_loop(0, count, one, 0)

        @pl.when(t == 1)
        def _():
            wait(gp_b.at[pl.ds(0, 56)], g_recv.at[0])
            row = iota((64, 64), 0)
            col = iota((64, 64), 1)
            turn = jnp.where(col == (row & 7) * 8 + (row >> 3), 1.0, 0.0)
            gp_c[...] = dot_f32(turn, gp_b[...])
            own = pl.ds(pl.multiple_of(z * 8, 8), 8)
            gp_d[own, :] = gp_c[0:8, :]
            for i in range(1, 8):
                remote(
                    gp_c.at[pl.ds(i * 8, 8)], gp_d.at[own], g_send.at[1], g_recv.at[1], dev_z(offsets[i])
                ).start()

        @pl.when(t == 2)
        def _():
            wait(gp_d.at[pl.ds(0, 56)], g_recv.at[1])
            row = iota((64, T), 0)
            expert = (((row & 7) >> 1) << 4) + ((row >> 3) << 1) + (row & 1)
            code = jnp.concatenate([meta[p, 0:8, :] for p in range(NZ)], axis=0)
            dense = jnp.zeros((64, T), F32)
            values = gp_d[...]
            for n in range(CAP):
                dense = dense + jnp.where(code == float(n), values[:, n : n + 1], 0.0)
            for k in range(8):
                hit = routes_ref[k : k + 1, :] == expert
                found = jnp.sum(jnp.where(hit, dense, 0.0), axis=0, keepdims=True)
                gprob_ref[k : k + 1, :] = found / probs_ref[k : k + 1, :]

        @pl.when(t == 3)
        def _():
            for n in range(3):
                wait(wpart.at[n], x_recv.at[n])
            mine = sent[mx, :, 0:WROWS, :].astype(F32)
            total = ((mine + wpart[0].astype(F32)) + wpart[1].astype(F32)) + wpart[2].astype(F32)
            ogate_ref[...] = jnp.transpose(total[0, 0:F])
            oup_ref[...] = jnp.transpose(total[1, 0:F])
            odown_ref[0 : F // 2, :] = total[0, F:WROWS]
            odown_ref[F // 2 :, :] = total[1, F:WROWS]

        return 0

    lax.fori_loop(0, 5, back, 0)

    for a, ref in ((0, out_ref), (1, gtok_ref)):
        for n in (1, 2):
            wait(zback.at[n, a], b_recv.at[n, a])
        total = psum[a] + zback[1, a].astype(F32) + zback[2, a].astype(F32)
        for q in range(Q):
            ref[:, q * DQ : (q + 1) * DQ] = total[q * T : (q + 1) * T, :].astype(BF16)

    wait(held.at[pl.ds(0, 2)], z_send.at[0])
    for i in range(1, 8):
        wait(meta.at[0], m_send.at[i])
    for i in range(8):
        wait(rows_in.at[i, :, pl.ds(0, 7 * BLK)], r_send.at[i])
    for i in range(1, 7):
        wait(held.at[i], b_send.at[i])
    for lo, n in ((0, 0), (256, 7)):
        wait(held.at[7, :, pl.ds(lo, 256)], b_send.at[n])
    for n in range(3):
        wait(wpart.at[n], x_send.at[n])
    for n in range(2):
        wait(gp_b.at[pl.ds(0, 56)], g_send.at[n])


def place(*refs):
    stage, sems = refs[12:18], refs[18]
    loads = [pltpu.make_async_copy(refs[n], stage[n], sems.at[0, n]) for n in range(6)]
    stores = [pltpu.make_async_copy(stage[n], refs[n + 6], sems.at[1, n]) for n in range(6)]
    for copy in loads:
        copy.start()
    for load, store in zip(loads, stores):
        load.wait()
        store.start()
    for copy in stores:
        copy.wait()


def shards(tokens, routes, gate_probs, cotangent, w_gate, w_up, w_down):
    vmem = pl.BlockSpec(memory_space=pltpu.VMEM)
    hbm = pl.BlockSpec(memory_space=pl.ANY)
    dma = pltpu.SemaphoreType.DMA
    results = pl.pallas_call(
        kernel,
        out_shape=(
            jax.ShapeDtypeStruct((T, D), BF16),
            jax.ShapeDtypeStruct((T, D), BF16),
            jax.ShapeDtypeStruct((8, T), F32),
            jax.ShapeDtypeStruct((F, F), F32),
            jax.ShapeDtypeStruct((F, F), F32),
            jax.ShapeDtypeStruct((F, F), F32),
        ),
        in_specs=[vmem] * 2 + [hbm] * 5,
        out_specs=(vmem,) * 6,
        scratch_shapes=[
            pltpu.VMEM((D, F), BF16),
            pltpu.VMEM((D, F), BF16),
            pltpu.VMEM((F, D), BF16),
            pltpu.VMEM((8, 2, TQ, DQ), BF16),
            pltpu.VMEM((4, 2, R, DQ), BF16),
            pltpu.VMEM((8, 2, R, DQ), BF16),
            pltpu.VMEM((8, 2, R, DQ), BF16),
            pltpu.VMEM((8 * ROWS, D), BF16),
            pltpu.VMEM((8 * ROWS, D), BF16),
            pltpu.VMEM((3, 8 * ROWS, F), BF16),
            pltpu.VMEM((8, 2, TQ, DQ), BF16),
            pltpu.VMEM((3, 2, WROWS, DQ), BF16),
            pltpu.VMEM((R, R), BF16),
            pltpu.VMEM((R, R), BF16),
            pltpu.VMEM((2, TQ, DQ), F32),
            pltpu.VMEM((8, 16, T), F32),
            pltpu.VMEM((8, 16, T), F32),
            pltpu.VMEM((8 * ROWS, 128), F32),
            pltpu.VMEM((64, 128), F32),
            pltpu.VMEM((64, 128), F32),
            pltpu.VMEM((64, 128), F32),
            pltpu.VMEM((64, 128), F32),
            dma((2, Q)),
            dma((3,)),
            dma((7,)),
            dma((8, 2)),
            dma((8,)),
            dma((8,)),
            dma((4, 2)),
            dma((8,)),
            dma((8,)),
            dma((8, 2)),
            dma((8,)),
            dma((8, 2)),
            dma((3,)),
            dma((3,)),
            dma((2,)),
            dma((2,)),
        ],
        compiler_params=pltpu.CompilerParams(
            collective_id=0, has_side_effects=True, vmem_limit_bytes=63 * 2**20
        ),
        cost_estimate=pl.CostEstimate(flops=20 * 10**9, bytes_accessed=10**7, transcendentals=10**6),
    )(routes.T, gate_probs.T, tokens, cotangent, w_gate[0], w_up[0], w_down[0])
    out, gtok, gprob, ogate, oup, odown = pl.pallas_call(
        place,
        out_shape=tuple(jax.ShapeDtypeStruct(v.shape, v.dtype) for v in results),
        in_specs=[hbm] * 6,
        out_specs=(hbm,) * 6,
        scratch_shapes=[pltpu.VMEM(v.shape, v.dtype) for v in results] + [dma((2, 6))],
    )(*results)
    return (out, gtok, gprob.T, ogate[None], oup[None], odown[None])


def solution(mesh):
    placed = (
        P(("mirror", "expert"), None),
        P(("mirror", "expert"), None),
        P(("mirror", "expert"), None),
        P(("mirror", "expert"), None),
        P("expert", None, None),
        P("expert", None, None),
        P("expert", None, None),
    )
    return jax.shard_map(
        shards,
        mesh=mesh,
        in_specs=placed,
        out_specs=(
            P(("mirror", "expert"), None),
            P(("mirror", "expert"), None),
            P(("mirror", "expert"), None),
            P("expert", "mirror", None),
            P("expert", "mirror", None),
            P("expert", None, "mirror"),
        ),
        check_vma=False,
    )
```

```python
import jax
import jax.numpy as jnp
from jax import lax
from jax.experimental import pallas as pl
from jax.experimental.pallas import tpu as pltpu
from jax.sharding import PartitionSpec as P

MESH = pl.DeviceIdType.MESH
F32 = jnp.float32
BF16 = jnp.bfloat16
NX, NY, NZ, NJ = 4, 4, 8, 8
T = 128
CAP = 20
Q = 4
DQ = 384
BLK = Q * CAP
R = NJ * BLK
TQ = Q * T
F = 384
D = 1536
ROWS = NJ * CAP
BATCH = 2 * ROWS
WROWS = F + F // 2


def dot(a, b):
    return jnp.dot(a, b, preferred_element_type=F32)


def dot_nt(a, b):
    return lax.dot_general(a, b, (((1,), (1,)), ((), ())), preferred_element_type=F32)


def dot_tn(a, b):
    return lax.dot_general(a, b, (((0,), (0,)), ((), ())), preferred_element_type=F32)


def dot_f32(a, b):
    return jnp.dot(a, b, preferred_element_type=F32, precision=lax.Precision.HIGHEST)


def iota(shape, dim):
    return lax.broadcasted_iota(jnp.int32, shape, dim)


def div20(v):
    return (v * 3277) >> 16


def wait(ref, sem):
    pltpu.make_async_copy(ref, ref, sem).wait()


def kernel(
    routes_ref, probs_ref, tok_hbm, cot_hbm, wg_hbm, wu_hbm, wd_hbm,
    out_ref, gtok_ref, gprob_ref, ogate_ref, oup_ref, odown_ref,
    wg, wu, wd, held, sent, rows_in, rows_back, xs, ss, hid, zback, wpart, perm, perm_t, psum,
    meta, meta_in, gs, gp_a, gp_b, gp_c, gp_d,
    w_out, o_sem, t_sem, w_sem, z_send, z_recv, m_send, m_recv, y_send, y_recv, r_send, r_recv,
    b_send, b_recv, x_send, x_recv, g_send, g_recv,
):
    mx = lax.axis_index("mirror")
    e = lax.axis_index("expert")
    y, z, core = e // 16, (e // 2) % 8, e % 2
    j = y * 2 + core

    def dev_j(other):
        return (mx, (other // 2) * 16 + z * 2 + other % 2)

    def dev_z(step):
        return (mx, y * 16 + ((z + step + 8) % 8) * 2 + core)

    def dev_x(step):
        return ((mx + step) % 4, e)

    offsets = [0, -1, 1, -2, 2, -3, 3, -4]

    barrier = pltpu.get_barrier_semaphore()
    for k in range(1, 8):
        pl.semaphore_signal(barrier, inc=1, device_id=dev_j((j + k) % 8), device_id_type=MESH)
        pl.semaphore_signal(barrier, inc=1, device_id=dev_z(k), device_id_type=MESH)
    for k in range(1, 4):
        pl.semaphore_signal(barrier, inc=1, device_id=dev_x(k), device_id_type=MESH)

    own = [
        pltpu.make_async_copy(src.at[:, pl.ds(q * DQ, DQ)], held.at[0, a, pl.ds(q * T, T)], t_sem.at[a, q])
        for a, src in enumerate((tok_hbm, cot_hbm))
        for q in range(Q)
    ]
    for copy in own:
        copy.start()

    weights = [
        pltpu.make_async_copy(src, dst, w_sem.at[n])
        for n, (src, dst) in enumerate(((wg_hbm, wg), (wu_hbm, wu), (wd_hbm, wd)))
    ]
    for copy in weights:
        copy.start()

    row = iota((64, T), 0)
    expert = (((row & 7) >> 1) << 4) + ((row >> 3) << 1) + (row & 1)
    member = jnp.zeros((64, T), F32)
    weight = jnp.zeros((64, T), F32)
    for k in range(8):
        hit = routes_ref[k : k + 1, :] == expert
        member = member + jnp.where(hit, 1.0, 0.0)
        weight = weight + jnp.where(hit, probs_ref[k : k + 1, :], 0.0)
    before = jnp.where(iota((T, T), 0) < iota((T, T), 1), 1.0, 0.0).astype(BF16)
    rank = dot(member.astype(BF16), before)
    code = jnp.where(member > 0.5, rank, -1.0)
    for p in range(NZ):
        meta[p, 0:8, :] = code[p * 8 : (p + 1) * 8, :]
        meta[p, 8:16, :] = weight[p * 8 : (p + 1) * 8, :]
    meta_in[0] = meta[z]

    def remote(src, dst, send, recv, device):
        return pltpu.make_async_remote_copy(
            src_ref=src, dst_ref=dst, send_sem=send, recv_sem=recv, device_id=device, device_id_type=MESH
        )

    r80 = iota((BLK, T), 0)
    q80 = div20(r80)
    slot80 = (r80 - q80 * CAP).astype(F32)

    def select(i, weighted):
        tops, lows = [], []
        for n in range(NJ):
            hit = meta_in[i, n : n + 1, :] == slot80
            if weighted:
                value = jnp.where(hit, meta_in[i, 8 + n : 9 + n, :], 0.0)
            else:
                value = jnp.where(hit, 1.0, 0.0)
            parts = [jnp.where(q80 == q, value, 0.0) for q in range(Q)]
            block = jnp.concatenate(parts, axis=1)
            top = block.astype(BF16)
            tops.append(top)
            if weighted:
                lows.append((block - top.astype(F32)).astype(BF16))
        top = jnp.concatenate(tops, axis=0)
        return (top, jnp.concatenate(lows, axis=0)) if weighted else (top,)

    def unit(i, a):
        s = i % 4
        wait(held.at[i, a], z_recv.at[i, a])

        @pl.when((i >= 1) & (i <= 4))
        def _():
            step = 2 * (i % 2) - 1
            remote(held.at[i, a], held.at[i + 2, a], z_send.at[i], z_recv.at[i + 2, a], dev_z(step)).start()

        @pl.when(i == 5)
        def _():
            half = held.at[5, a, pl.ds(0, 256)]
            remote(half, held.at[7, a, pl.ds(0, 256)], z_send.at[5], z_recv.at[7, a], dev_z(1)).start()

        @pl.when(i == 6)
        def _():
            half = held.at[6, a, pl.ds(256, 256)]
            remote(half, held.at[7, a, pl.ds(256, 256)], z_send.at[6], z_recv.at[7, a], dev_z(-1)).start()

        if a == 0:

            wait(meta_in.at[i], m_recv.at[i])

        @pl.when(i >= 4)
        def _():
            wait(sent.at[s, a, pl.ds(0, 7 * BLK)], y_send.at[s, a])

        pick(i, a)
        send_out(i, a)

    def pick(i, a):
        s = i % 4
        source = held[i, a]
        picked = sum(dot(m, source) for m in select(i, a == 1))
        sent[s, a] = picked.astype(BF16)
        mine = pl.ds(pl.multiple_of(j * BLK, 16), BLK)
        rows_in[i, a, mine, :] = sent[s, a, mine, :]

    def send_out(i, a):
        s = i % 4
        mine = pl.ds(pl.multiple_of(j * BLK, 16), BLK)

        def send(k, _):
            other = (j + k) % 8
            theirs = pl.ds(pl.multiple_of(other * BLK, 16), BLK)
            remote(
                sent.at[s, a, theirs], rows_in.at[i, a, mine], y_send.at[s, a], y_recv.at[i], dev_j(other)
            ).start()
            return 0

        lax.fori_loop(1, 8, send, 0)

    def compute(c):
        base = pl.multiple_of(c * BATCH, 16)
        slots = (2 * c + 1, (2 * c + 2) % 8)
        for m, i in enumerate(slots):
            wait(rows_in.at[i, :, pl.ds(0, 7 * BLK)], y_recv.at[i])
            for a, store in ((0, xs), (1, ss)):
                flat = dot(perm[...], rows_in[i, a]).astype(BF16)
                for q in range(Q):
                    store[pl.ds(base + m * ROWS, ROWS), q * DQ : (q + 1) * DQ] = flat[
                        q * ROWS : (q + 1) * ROWS, :
                    ]
        batch = pl.ds(base, BATCH)
        x = xs[batch, :]
        pre_gate = dot(x, wg[...])
        pre_up = dot(x, wu[...])
        sig = jax.nn.sigmoid(pre_gate)
        hidden = (pre_gate * sig * pre_up).astype(BF16)
        grad_hidden = dot_nt(ss[batch, :], wd[...])
        grad_gate = (grad_hidden * pre_up * sig * (1.0 + pre_gate * (1.0 - sig))).astype(BF16)
        grad_up = (grad_hidden * pre_gate * sig).astype(BF16)
        hid[0, batch, :] = grad_gate
        hid[1, batch, :] = grad_up
        hid[2, batch, :] = hidden
        total = jnp.sum(grad_hidden * hidden.astype(F32), axis=1, keepdims=True)
        gs[batch, :] = jnp.broadcast_to(total, (BATCH, 128))
        out = dot(hidden, wd[...]).astype(BF16)
        for m, i in enumerate(slots):
            part = out[m * ROWS : (m + 1) * ROWS, :]
            flat = jnp.concatenate([part[:, q * DQ : (q + 1) * DQ] for q in range(Q)], axis=0)
            rows_in[i, 0] = dot(perm_t[...], flat).astype(BF16)
        grad = (dot_nt(grad_gate, wg[...]) + dot_nt(grad_up, wu[...])).astype(BF16)
        for m, i in enumerate(slots):
            part = grad[m * ROWS : (m + 1) * ROWS, :]
            flat = jnp.concatenate([part[:, q * DQ : (q + 1) * DQ] for q in range(Q)], axis=0)
            rows_in[i, 1] = dot(perm_t[...], flat).astype(BF16)

    def give_back(i, a):
        mine = pl.ds(pl.multiple_of(j * BLK, 16), BLK)
        rows_back[i, a, mine, :] = rows_in[i, a, mine, :]

        def send(k, _):
            other = (j + k) % 8
            theirs = pl.ds(pl.multiple_of(other * BLK, 16), BLK)
            remote(
                rows_in.at[i, a, theirs], rows_back.at[i, a, mine], r_send.at[i], r_recv.at[i, a], dev_j(other)
            ).start()
            return 0

        lax.fori_loop(1, 8, send, 0)

    def give(slots, a):
        def one(n, _):
            give_back(slots - n, a)
            return 0

        return one

    def bounds(g):
        return jnp.minimum(jnp.maximum(2 * g - 1, 0), 8), jnp.minimum(2 * g + 1, 8)

    def make_perms():
        lane = iota((R, R), 1)
        r = iota((R, R), 0)
        r20 = div20(r)
        slot_of = r - r20 * 20
        perm[...] = jnp.where(lane == (r20 & 7) * BLK + (r20 >> 3) * CAP + slot_of, 1.0, 0.0).astype(BF16)
        perm_t[...] = jnp.where(
            lane == (r20 & 3) * ROWS + (r20 >> 2) * CAP + slot_of, 1.0, 0.0
        ).astype(BF16)


    def group(g, _):
        first, last = bounds(g)
        for a in range(2):

            def one(i, _, a=a):
                unit(i, a)
                return 0

            lax.fori_loop(first, last, one, 0)

        @pl.when(g == 2)
        def _():
            for copy in weights:
                copy.wait()

        @pl.when(g >= 2)
        def _():
            compute(g - 2)

        @pl.when(g == 4)
        def _():
            for a in range(2):
                give_back(6, a)

        @pl.when(g == 5)
        def _():
            for i in (7, 5):
                for a in range(2):
                    give_back(i, a)

        return 0

    for a in range(2):
        for copy in own[a * Q : (a + 1) * Q]:
            copy.wait()
        pick(0, a)
    pl.semaphore_wait(barrier, 17)
    send_out(0, 0)
    for a in range(2):
        for slot, step in ((1, 1), (2, -1)):
            remote(held.at[0, a], held.at[slot, a], z_send.at[0], z_recv.at[slot, a], dev_z(step)).start()
        if a == 0:
            for i in range(1, 8):
                to = -offsets[i]
                remote(
                    meta.at[(z + to + 8) % 8], meta_in.at[i], m_send.at[i], m_recv.at[i], dev_z(to)
                ).start()
    send_out(0, 1)
    make_perms()
    lax.fori_loop(1, 6, group, 0)

    row = iota((8 * ROWS, 128), 0)
    lanes = iota((8 * ROWS, 128), 1)
    spread = jnp.where(lanes == row - div20(row) * CAP, gs[...], 0.0)
    row = iota((64, 8 * ROWS), 0)
    block = div20(iota((64, 8 * ROWS), 1))
    pick = jnp.where(row == (block & 7) * 8 + (((block >> 3) + 1) & 7), 1.0, 0.0)
    gp_a[...] = dot_f32(pick, spread)
    tile = pl.ds(pl.multiple_of(j * 8, 8), 8)
    gp_b[tile, :] = gp_a[tile, :]

    def send_gp(k, _):
        other = (j + k) % 8
        theirs = pl.ds(pl.multiple_of(other * 8, 8), 8)
        remote(gp_a.at[theirs], gp_b.at[tile], g_send.at[0], g_recv.at[0], dev_j(other)).start()
        return 0

    lax.fori_loop(1, 8, send_gp, 0)

    for s in range(4):
        for a in range(2):
            wait(sent.at[s, a, pl.ds(0, 7 * BLK)], y_send.at[s, a])

    def grads(n, _):
        for kind, store in ((0, xs), (1, xs), (2, ss)):
            cols = pl.ds(pl.multiple_of(n * DQ, 128), DQ)
            part = dot_tn(hid[kind], store[:, cols]).astype(BF16)
            if kind == 0:
                sent[n, 0, 0:F, :] = part
            elif kind == 1:
                sent[n, 1, 0:F, :] = part
            else:
                sent[n, 0, F:WROWS, :] = part[0 : F // 2, :]
                sent[n, 1, F:WROWS, :] = part[F // 2 :, :]
        return 0

    lax.fori_loop(0, 4, grads, 0)
    for k in range(1, 4):
        other = (mx + k) % 4
        remote(
            sent.at[other, :, pl.ds(0, WROWS)],
            wpart.at[k - 1],
            x_send.at[k - 1],
            x_recv.at[k - 1],
            dev_x(k),
        ).start()

    def back_unit(i, a):
        wait(rows_back.at[i, a, pl.ds(0, 7 * BLK)], r_recv.at[i, a])
        psum[a] = sum(dot_tn(m, rows_back[i, a]) for m in select(i, a == 0))

        @pl.when((i >= 1) & (i <= 4))
        def _():
            wait(zback.at[i + 2, a], b_recv.at[i + 2, a])
            psum[a] = psum[a] + zback[i + 2, a].astype(F32)

        @pl.when(i == 5)
        def _():
            wait(zback.at[7, a, pl.ds(0, 256)], b_recv.at[0, a])
            psum[a, 0:256, :] = psum[a, 0:256, :] + zback[7, a, 0:256, :].astype(F32)

        @pl.when(i == 6)
        def _():
            wait(zback.at[7, a, pl.ds(256, 256)], b_recv.at[7, a])
            psum[a, 256:512, :] = psum[a, 256:512, :] + zback[7, a, 256:512, :].astype(F32)

        if a == 0:

            @pl.when((i >= 1) & (i <= 4))
            def _():
                wait(held.at[i], z_send.at[i])

            @pl.when((i >= 5) & (i <= 6))
            def _():
                wait(held.at[i, :, pl.ds(0, 256)], z_send.at[i])

        @pl.when(i >= 1)
        def _():
            held[i, a] = psum[a].astype(BF16)

        @pl.when((i >= 1) & (i <= 6))
        def _():
            step = 1 - 2 * (i % 2)
            remote(held.at[i, a], zback.at[i, a], b_send.at[i], b_recv.at[i, a], dev_z(step)).start()

        @pl.when(i == 7)
        def _():
            for lo, step, n in ((0, -1, 0), (256, 1, 7)):
                half = (7, a, pl.ds(lo, 256))
                remote(held.at[half], zback.at[half], b_send.at[n], b_recv.at[n, a], dev_z(step)).start()

    def back(t, _):
        first = jnp.where(t == 0, 7, jnp.where(t == 1, 6, jnp.where(t == 4, 0, 4)))
        plain = jnp.where(t == 1, 2, 1)

        @pl.when(t == 1)
        def _():
            lax.fori_loop(0, 4, give(4, 0), 0)

        @pl.when(t == 2)
        def _():
            lax.fori_loop(0, 4, give(4, 1), 0)

        @pl.when(t == 3)
        def _():
            for a in range(2):
                give_back(0, a)

        for a in range(2):
            count = jnp.where(t == 2 + a, 4, jnp.where(t == 3 - a, 0, plain))

            def one(n, _, a=a):
                back_unit(first - n, a)
                return 0

            lax.fori_loop(0, count, one, 0)

        @pl.when(t == 1)
        def _():
            wait(gp_b.at[pl.ds(0, 56)], g_recv.at[0])
            row = iota((64, 64), 0)
            col = iota((64, 64), 1)
            turn = jnp.where(col == (row & 7) * 8 + (row >> 3), 1.0, 0.0)
            gp_c[...] = dot_f32(turn, gp_b[...])
            own = pl.ds(pl.multiple_of(z * 8, 8), 8)
            gp_d[own, :] = gp_c[0:8, :]
            for i in range(1, 8):
                remote(
                    gp_c.at[pl.ds(i * 8, 8)], gp_d.at[own], g_send.at[1], g_recv.at[1], dev_z(offsets[i])
                ).start()

        @pl.when(t == 2)
        def _():
            wait(gp_d.at[pl.ds(0, 56)], g_recv.at[1])
            row = iota((64, T), 0)
            expert = (((row & 7) >> 1) << 4) + ((row >> 3) << 1) + (row & 1)
            code = jnp.concatenate([meta[p, 0:8, :] for p in range(NZ)], axis=0)
            dense = jnp.zeros((64, T), F32)
            values = gp_d[...]
            for n in range(CAP):
                dense = dense + jnp.where(code == float(n), values[:, n : n + 1], 0.0)
            for k in range(8):
                hit = routes_ref[k : k + 1, :] == expert
                found = jnp.sum(jnp.where(hit, dense, 0.0), axis=0, keepdims=True)
                gprob_ref[k : k + 1, :] = found / probs_ref[k : k + 1, :]

        @pl.when(t == 3)
        def _():
            for n in range(3):
                wait(wpart.at[n], x_recv.at[n])
            mine = sent[mx, :, 0:WROWS, :].astype(F32)
            total = ((mine + wpart[0].astype(F32)) + wpart[1].astype(F32)) + wpart[2].astype(F32)
            w_out[0] = jnp.transpose(total[0, 0:F])
            w_out[1] = jnp.transpose(total[1, 0:F])
            w_out[2, 0 : F // 2, :] = total[0, F:WROWS]
            w_out[2, F // 2 :, :] = total[1, F:WROWS]
            for n, ref in enumerate((ogate_ref, oup_ref, odown_ref)):
                pltpu.make_async_copy(w_out.at[n], ref, o_sem.at[n]).start()

        return 0

    lax.fori_loop(0, 5, back, 0)

    for a, ref in ((0, out_ref), (1, gtok_ref)):
        for n in (1, 2):
            wait(zback.at[n, a], b_recv.at[n, a])
        total = psum[a] + zback[1, a].astype(F32) + zback[2, a].astype(F32)
        for q in range(Q):
            ref[:, q * DQ : (q + 1) * DQ] = total[q * T : (q + 1) * T, :].astype(BF16)

    for n in range(3):
        wait(w_out.at[n], o_sem.at[n])
    wait(held.at[pl.ds(0, 2)], z_send.at[0])
    for i in range(1, 8):
        wait(meta.at[0], m_send.at[i])
    for i in range(8):
        wait(rows_in.at[i, :, pl.ds(0, 7 * BLK)], r_send.at[i])
    for i in range(1, 7):
        wait(held.at[i], b_send.at[i])
    for lo, n in ((0, 0), (256, 7)):
        wait(held.at[7, :, pl.ds(lo, 256)], b_send.at[n])
    for n in range(3):
        wait(wpart.at[n], x_send.at[n])
    for n in range(2):
        wait(gp_b.at[pl.ds(0, 56)], g_send.at[n])


def place(*refs):
    stage, sems = refs[12:18], refs[18]
    loads = [pltpu.make_async_copy(refs[n], stage[n], sems.at[0, n]) for n in range(6)]
    stores = [pltpu.make_async_copy(stage[n], refs[n + 6], sems.at[1, n]) for n in range(6)]
    for copy in loads:
        copy.start()
    for load, store in zip(loads, stores):
        load.wait()
        store.start()
    for copy in stores:
        copy.wait()


def shards(tokens, routes, gate_probs, cotangent, w_gate, w_up, w_down):
    vmem = pl.BlockSpec(memory_space=pltpu.VMEM)
    hbm = pl.BlockSpec(memory_space=pl.ANY)
    dma = pltpu.SemaphoreType.DMA
    results = pl.pallas_call(
        kernel,
        out_shape=(
            jax.ShapeDtypeStruct((T, D), BF16),
            jax.ShapeDtypeStruct((T, D), BF16),
            jax.ShapeDtypeStruct((8, T), F32),
            jax.ShapeDtypeStruct((F, F), F32),
            jax.ShapeDtypeStruct((F, F), F32),
            jax.ShapeDtypeStruct((F, F), F32),
        ),
        in_specs=[vmem] * 2 + [hbm] * 5,
        out_specs=(vmem,) * 3 + (hbm,) * 3,
        scratch_shapes=[
            pltpu.VMEM((D, F), BF16),
            pltpu.VMEM((D, F), BF16),
            pltpu.VMEM((F, D), BF16),
            pltpu.VMEM((8, 2, TQ, DQ), BF16),
            pltpu.VMEM((4, 2, R, DQ), BF16),
            pltpu.VMEM((8, 2, R, DQ), BF16),
            pltpu.VMEM((8, 2, R, DQ), BF16),
            pltpu.VMEM((8 * ROWS, D), BF16),
            pltpu.VMEM((8 * ROWS, D), BF16),
            pltpu.VMEM((3, 8 * ROWS, F), BF16),
            pltpu.VMEM((8, 2, TQ, DQ), BF16),
            pltpu.VMEM((3, 2, WROWS, DQ), BF16),
            pltpu.VMEM((R, R), BF16),
            pltpu.VMEM((R, R), BF16),
            pltpu.VMEM((2, TQ, DQ), F32),
            pltpu.VMEM((8, 16, T), F32),
            pltpu.VMEM((8, 16, T), F32),
            pltpu.VMEM((8 * ROWS, 128), F32),
            pltpu.VMEM((64, 128), F32),
            pltpu.VMEM((64, 128), F32),
            pltpu.VMEM((64, 128), F32),
            pltpu.VMEM((64, 128), F32),
            pltpu.VMEM((3, F, F), F32),
            dma((3,)),
            dma((2, Q)),
            dma((3,)),
            dma((7,)),
            dma((8, 2)),
            dma((8,)),
            dma((8,)),
            dma((4, 2)),
            dma((8,)),
            dma((8,)),
            dma((8, 2)),
            dma((8,)),
            dma((8, 2)),
            dma((3,)),
            dma((3,)),
            dma((2,)),
            dma((2,)),
        ],
        compiler_params=pltpu.CompilerParams(
            collective_id=0, has_side_effects=True, vmem_limit_bytes=63 * 2**20
        ),
        cost_estimate=pl.CostEstimate(flops=20 * 10**9, bytes_accessed=10**7, transcendentals=10**6),
    )(routes.T, gate_probs.T, tokens, cotangent, w_gate[0], w_up[0], w_down[0])
    out, gtok, gprob, ogate, oup, odown = pl.pallas_call(
        place,
        out_shape=tuple(jax.ShapeDtypeStruct(v.shape, v.dtype) for v in results),
        in_specs=[hbm] * 6,
        out_specs=(hbm,) * 6,
        scratch_shapes=[pltpu.VMEM(v.shape, v.dtype) for v in results] + [dma((2, 6))],
    )(*results)
    return (out, gtok, gprob.T, ogate[None], oup[None], odown[None])


def solution(mesh):
    placed = (
        P(("mirror", "expert"), None),
        P(("mirror", "expert"), None),
        P(("mirror", "expert"), None),
        P(("mirror", "expert"), None),
        P("expert", None, None),
        P("expert", None, None),
        P("expert", None, None),
    )
    return jax.shard_map(
        shards,
        mesh=mesh,
        in_specs=placed,
        out_specs=(
            P(("mirror", "expert"), None),
            P(("mirror", "expert"), None),
            P(("mirror", "expert"), None),
            P("expert", "mirror", None),
            P("expert", "mirror", None),
            P("expert", None, "mirror"),
        ),
        check_vma=False,
    )
```
